32 devices in a mesh: tp: 2 (over core), dp: 16 (over z, y, x).
Axes of the slice: x: 2, y: 2, z: 4, core: 2. Of those that a mesh axis runs over, the one named last changes fastest.
Arguments:
- hidden: bfloat16 [32768, 8192], P('dp', 'tp')
- norm_gain: bfloat16 [8192], P('tp'), may hold values from 0.099609375 to 1.8984375
- projection: bfloat16 [8192, 1024], P('tp'), may hold values from -0.0625 to 0.0625
- centroids: bfloat16 [65536, 1024], P('dp'), may hold values from -6 to 6
- owners: int32 [32768, 1], P(('dp', 'tp')), may hold values from 0 to 15; in each aligned block of 1024 rows (0 to 1023, 1024 to 2047, ...) at most 192 rows name the same one
- local_list: int32 [32768], P(('dp', 'tp')), may hold values from 0 to 4095
- slot_table: int32 [32, 3072], P(('dp', 'tp')), may hold values from 0 to 3071, each once within a row
Outputs:
- codes: bfloat16 [98304, 1024], P(('dp', 'tp'))
The draws below stay inside these ranges and needn't reach their ends.
Inputs may be any that keep to these rules, and one draw needn't show every extreme that they name: `owners`: in the 1024 tokens of one device no owner is named more than 192 times; some device names an owner exactly 192 times. `slot_table`: each row is a permutation of 0 to 3071.
All inputs are finite; a program needn't handle non-finite values.
Results may differ from the reference program's by a relative error of at most 0.011.
Values may be sent and summed in bfloat16 or wider, within the bound.
No kernel may reach another device: no remote copies, remote signals or barrier semaphores. Data moves between devices by JAX's collectives and lax.ppermute only.
A program may use at most 128 MiB of HBM per device.

```python
import math
import jax
import jax.numpy as jnp
import numpy as np
from jax import lax

D = 8192
KD = 1024
LISTS = 65536
TOK_GROUP = 2048
TOKENS = 32768
ROWS = 1024
CAP = 192
BUF = 3072
LISTS_DEV = 4096
N_TP = 2
N_DP = 16


def draw_hidden(key, part):
    key_base, key_col, key_row = jax.random.split(key, 3)
    col_pos = jnp.arange(D, dtype=jnp.float32) / D
    col_scale = jnp.exp(math.log(10.0) * (0.6 * col_pos + 0.4 * jax.random.uniform(key_col, (D,), jnp.float32)))
    base = jax.random.normal(key_base, (TOKENS, D), jnp.float32)
    row_scale = jnp.exp(math.log(10.0) * jax.random.uniform(key_row, (TOKENS, 1), jnp.float32))
    values = 0.3 * base * col_scale[None, :] * row_scale
    return values.astype(jnp.bfloat16)


def touch_ends(values, key, low, top_value):
    index_at = [jax.random.randint(jax.random.fold_in(key, axis), (), 0, length) for axis, length in enumerate(values.shape)]
    main_axis = values.shape.index(max(values.shape))
    next_to = index_at[:main_axis] + [(index_at[main_axis] + 1) % values.shape[main_axis]] + index_at[main_axis + 1:]
    return values.at[tuple(index_at)].set(low).at[tuple(next_to)].set(top_value)


def level_of(key, extent, shards, smallest, top_value):
    level = 1.0
    for position, parts in shards:
        steps = jax.random.uniform(jax.random.fold_in(jax.random.fold_in(key, 6), position), (parts,), jnp.float32, smallest / len(shards), top_value / len(shards))
        level = level * jnp.repeat(jnp.exp(steps), extent[position] // parts).reshape((-1,) + (1,) * (len(extent) - 1 - position))
    return level


def deal_out(rng, own, number, rows, amount, top, bound, lean):
    ranking = jax.random.permutation(rng, amount)
    heavy_load, common = shares(amount, rows * top, bound, lean, True), shares(amount, rows * top, bound, lean, False)
    places = jnp.arange(amount)

    def named(tallies, rotation):
        used = int((tallies > 0).sum())
        fixed = max(1, used // 4)
        passed = fixed + (places - fixed + rotation * (used - fixed)) % max(1, amount - fixed)
        return jnp.zeros((amount,), jnp.int32).at[ranking[jnp.where(places < fixed, places, passed)]].set(jnp.asarray(tallies, jnp.int32))

    tallies = jnp.where(number % 4 == 0, named(heavy_load, number // 4), named(common, number - number // 4 - 1))
    mixed = jax.random.permutation(jax.random.fold_in(own, 3), amount)
    source_of, receiver = mixed[0:amount // 2 * 2:2], mixed[1:amount // 2 * 2:2]
    margin = jnp.minimum(tallies[source_of] - 1, bound - tallies[receiver]) // 2
    margin = jnp.where((source_of == ranking[0]) | (receiver == ranking[0]) | (tallies[receiver] == 0), 0, jnp.maximum(margin, 0))
    passed = jax.random.randint(jax.random.fold_in(own, 4), (amount // 2,), 0, 1 << 20) % (margin + 1)
    tallies = tallies.at[source_of].add(-passed).at[receiver].add(passed)
    members = jnp.searchsorted(jnp.cumsum(tallies), jnp.arange(rows * top), side="right").astype(jnp.int32)
    grid = members.reshape(top, rows).T
    grid = grid[jax.random.permutation(jax.random.fold_in(own, 1), rows)]
    rotation = jax.random.randint(jax.random.fold_in(own, 2), (rows, 1), 0, top)
    return jnp.take_along_axis(grid, (jnp.arange(top)[None, :] + rotation) % top, axis=1)


def shares(count, total, limit, lean, full):
    portions = [(1 << 20) // math.isqrt(grade ** lean) + 1 for grade in range(1, count + 1)]
    largest = limit if full else min(limit, max(-(-total // count), total * portions[0] // sum(portions)))
    least = 1 if total - largest >= count - 1 else 0
    counts, surplus = [largest] + [least] * (count - 1), total - largest - least * (count - 1)
    while surplus > 0:
        candidates = [i for i in range(1, count) if counts[i] < largest] or [i for i in range(1, count) if counts[i] < limit]
        mass, budget = sum([portions[i] for i in candidates]), surplus
        for i in candidates:
            addition = min(limit - counts[i], max(1, budget * portions[i] // mass), surplus)
            counts[i] = counts[i] + addition
            surplus = surplus - addition
    return np.array(counts)


def scatter_about(own_key, extent, deviation, most, cuts=(), held_as=jnp.bfloat16):
    entries = deviation * jax.random.normal(own_key, extent, jnp.float32)
    if cuts:
        entries = entries * level_of(own_key, extent, cuts, -0.22, 0.18)
    return jnp.clip(entries, -most, most).astype(held_as)


def setup_inputs(seed: int = 0) -> dict:
    keys = jax.random.split(jax.random.key(seed), 8)
    hidden = draw_hidden(jax.random.fold_in(keys[7], 71), 0)
    norm_gain = jnp.clip(1.0 + 0.18 * jax.random.normal(keys[1], (D,), jnp.float32), 0.099609375, 1.8984375).astype(jnp.bfloat16)
    projection = scatter_about(keys[2], (D, KD), D ** -0.5, 0.0625, ((0, 2),))
    centroids = scatter_about(keys[3], (LISTS, KD), 1.0, 6.0, ((0, 16),))
    owners_keys = jax.random.split(jax.random.fold_in(keys[4], 1), TOKENS // ROWS)
    owners_turns = jax.random.permutation(jax.random.fold_in(keys[4], 3), TOKENS // ROWS)
    owners = jax.vmap(lambda own, number: deal_out(jax.random.fold_in(keys[4], 2), own, number, ROWS, N_DP, 1, CAP, 2))(owners_keys, owners_turns).reshape((TOKENS, 1))
    local_list = touch_ends(jax.random.randint(keys[5], (TOKENS,), 0, LISTS_DEV), jax.random.fold_in(keys[5], 1), 0, LISTS_DEV - 1).astype(jnp.int32)
    slot_table = jax.vmap(lambda own: jax.random.permutation(own, BUF))(jax.random.split(keys[6], (N_DP * N_TP))).reshape((N_DP * N_TP, BUF)).astype(jnp.int32)
    return dict(hidden=hidden, norm_gain=norm_gain, projection=projection, centroids=centroids, owners=owners, local_list=local_list, slot_table=slot_table)


EPSILON = 1e-05

def group_keys(group, norm_gain, projection):
    values = group.astype(jnp.float32)
    energy = lax.optimization_barrier(jnp.sum(values * values, axis=1))
    inv_rms = lax.rsqrt(energy / D + EPSILON)
    normed = (values * norm_gain.astype(jnp.float32)[None, :] * inv_rms[:, None]).astype(jnp.bfloat16)
    pieces = normed.reshape(TOK_GROUP, N_TP, D // N_TP).astype(jnp.float32)
    weights = projection.reshape(N_TP, D // N_TP, KD).astype(jnp.float32)
    partial_keys = jnp.einsum('tjd,jdk->jtk', pieces, weights)
    rounded = lax.optimization_barrier(partial_keys.astype(jnp.bfloat16))
    return lax.optimization_barrier(jnp.sum(rounded.astype(jnp.float32), axis=0))

def reference(hidden, norm_gain, projection, centroids, owners, local_list, slot_table):
    grouped = hidden.reshape(N_DP, TOK_GROUP, D)
    key_rows = lax.map(lambda part_rows: group_keys(part_rows, norm_gain, projection), grouped).reshape(TOKENS, KD)
    owner_ids = owners[:, 0].astype(jnp.int32)
    onehot = (owner_ids[:, None] == jnp.arange(N_DP, dtype=jnp.int32)[None, :]).astype(jnp.int32)
    running = jnp.cumsum(onehot.reshape(N_DP * N_TP, ROWS, N_DP), axis=1).reshape(TOKENS, N_DP)
    rank_in = lax.optimization_barrier(jnp.sum(onehot * (running - 1), axis=1)).astype(jnp.int32)
    device_ids = jnp.arange(TOKENS, dtype=jnp.int32) // ROWS
    source_dp = device_ids // N_TP
    source_tp = device_ids % N_TP
    target = owner_ids * N_TP + source_tp
    arrival = source_dp * CAP + rank_in
    slot_ids = slot_table[target, arrival].astype(jnp.int32)
    global_list = owner_ids * LISTS_DEV + local_list.astype(jnp.int32)
    residual = (key_rows - centroids[global_list].astype(jnp.float32)).astype(jnp.bfloat16)
    codes = jnp.zeros((N_DP * N_TP * BUF, KD), jnp.bfloat16).at[target * BUF + slot_ids].set(residual)
    return codes
```

```python
import functools

import jax
import jax.numpy as jnp
from jax import lax
from jax.experimental import pallas as pl
from jax.experimental.pallas import tpu as pltpu
from jax.sharding import PartitionSpec as P

D = 8192
EPSILON = 1e-05
LANES = 128
MIB = 1024 * 1024
F32 = jnp.float32
BF16 = jnp.bfloat16
I32 = jnp.int32


def iota(shape, dim):
    return lax.broadcasted_iota(I32, shape, dim)


def fit(total, wanted):
    best = 16
    for size in range(16, min(total, wanted) + 1, 16):
        if total % size == 0:
            best = size
    return best


def params(mib):
    return pltpu.CompilerParams(vmem_limit_bytes=mib * MIB)


def partial_kernel(which, hidden, gain, projection, out, total, squares):
    step = pl.program_id(0)
    rows, depth = hidden.shape
    tile = fit(rows, 256)

    @pl.when(step == 0)
    def _():
        total[...] = jnp.zeros_like(total)
        squares[...] = jnp.zeros_like(squares)

    @pl.loop(0, rows // tile)
    def _(i):
        at = pl.ds(pl.multiple_of(i * tile, tile), tile)
        block = hidden[at, :]
        total[at, :] += jnp.dot(block * gain[...], projection[...], preferred_element_type=F32)
        wide = block.astype(F32)
        wide = wide * wide
        part = wide[:, :LANES]
        for lane in range(LANES, depth, LANES):
            part = part + wide[:, lane : lane + LANES]
        squares[at, :] += part

    @pl.when(step == pl.num_programs(0) - 1)
    def _():
        width = total.shape[1]

        @pl.loop(0, rows // tile)
        def _(i):
            at = pl.ds(pl.multiple_of(i * tile, tile), tile)
            out[at, :width] = total[at, :].astype(BF16)
            energy = squares[at, :]
            high = energy.astype(BF16)
            wide = high.astype(F32)
            out[at, width : width + LANES] = high
            out[at, width + LANES :] = jnp.where(wide < 3e38, energy - wide, 0.0).astype(BF16)


def partial_keys(which, hidden, gain, projection, rows):
    depth, width = projection.shape
    block = 1024
    return pl.pallas_call(
        partial_kernel,
        grid_spec=pltpu.PrefetchScalarGridSpec(
            num_scalar_prefetch=1,
            grid=(depth // block,),
            in_specs=[
                pl.BlockSpec((rows, block), lambda k, w: (w[0], k)),
                pl.BlockSpec((1, block), lambda k, w: (0, k)),
                pl.BlockSpec((block, width), lambda k, w: (k, 0)),
            ],
            out_specs=pl.BlockSpec((rows, width + 2 * LANES), lambda k, w: (0, 0)),
            scratch_shapes=[pltpu.VMEM((rows, width), F32), pltpu.VMEM((rows, LANES), F32)],
        ),
        out_shape=jax.ShapeDtypeStruct((rows, width + 2 * LANES), BF16),
        compiler_params=params(32),
        cost_estimate=pl.CostEstimate(
            flops=2 * rows * depth * width,
            bytes_accessed=2 * (rows * depth + depth * width + rows * width),
            transcendentals=0,
        ),
        name="partial_keys",
    )(which, hidden, gain, projection)


def route_kernel(n_dp, cap, owners, lists, place, listed):
    rows = owners.shape[1]
    n_own = 128 if n_dp <= 128 else n_dp
    hot = iota((n_own, rows), 0) == owners[...]
    onehot = hot.astype(F32).astype(BF16)
    before = (iota((rows, rows), 0) < iota((rows, rows), 1)).astype(F32).astype(BF16)
    ranks = jnp.dot(onehot, before, preferred_element_type=F32)
    rank = jnp.sum(jnp.where(hot, ranks, 0.0), axis=0, keepdims=True).astype(I32)
    place[...] = jnp.broadcast_to(owners[...] * cap + rank, place.shape)
    at_rank = (iota((listed.shape[1], rows), 0) == rank).astype(F32).astype(BF16)
    high = (lists[...] // 64).astype(F32)
    low = (lists[...] % 64).astype(F32)

    def by_owner(values):
        picked = jnp.where(hot, values, 0.0).astype(BF16)
        return lax.dot_general(picked, at_rank, (((1,), (1,)), ((), ())), preferred_element_type=F32)

    live = by_owner(jnp.ones_like(high))
    ids = by_owner(high) * 64.0 + by_owner(low)
    found = jnp.where(live > 0.5, ids, -1.0).astype(I32)
    listed[...] = found[:n_dp, :]


def route(owners, lists, n_dp, cap):
    rows = owners.shape[1]
    wide = -(-cap // LANES) * LANES
    return pl.pallas_call(
        functools.partial(route_kernel, n_dp, cap),
        out_shape=(
            jax.ShapeDtypeStruct((8, rows), I32),
            jax.ShapeDtypeStruct((n_dp, wide), I32),
        ),
        compiler_params=params(32),
        cost_estimate=pl.CostEstimate(
            flops=2 * rows * rows * 128, bytes_accessed=rows * 64, transcendentals=0
        ),
        name="route",
    )(owners, lists)


def pack_kernel(own, other, place, out, keys):
    width = keys.shape[1]
    rows = keys.shape[0]
    step = pl.program_id(0)

    @pl.when(step == 0)
    def _():
        tile = fit(rows, 128)

        @pl.loop(0, rows // tile)
        def _(i):
            at = pl.ds(pl.multiple_of(i * tile, tile), tile)
            parts = own[at, width:].astype(F32) + other[at, width:].astype(F32)
            energy = jnp.sum(parts, axis=1, keepdims=True)
            scale = lax.rsqrt(energy * (1.0 / D) + EPSILON)
            terms = own[at, :width].astype(F32) + other[at, :width].astype(F32)
            keys[at, :] = jnp.where(scale > 0.0, terms * scale, 0.0).astype(BF16)

    size = out.shape[0]
    onehot = (iota((size, rows), 0) + step * size == place[0:1, :]).astype(F32).astype(BF16)
    out[...] = jnp.dot(onehot, keys[...], preferred_element_type=F32).astype(BF16)


def pack(own, other, place, total):
    rows = own.shape[0]
    width = own.shape[1] - 2 * LANES
    tile = fit(total, 512)
    return pl.pallas_call(
        pack_kernel,
        grid=(total // tile,),
        in_specs=[
            pl.BlockSpec((rows, width + 2 * LANES), lambda i: (0, 0)),
            pl.BlockSpec((rows, width + 2 * LANES), lambda i: (0, 0)),
            pl.BlockSpec((8, rows), lambda i: (0, 0)),
        ],
        out_specs=pl.BlockSpec((tile, width), lambda i: (i, 0)),
        out_shape=jax.ShapeDtypeStruct((total, width), BF16),
        scratch_shapes=[pltpu.VMEM((rows, width), BF16)],
        compiler_params=params(40),
        cost_estimate=pl.CostEstimate(
            flops=2 * total * rows * width,
            bytes_accessed=2 * width * (2 * rows + total),
            transcendentals=rows,
        ),
        name="pack_keys",
    )(own, other, place)


def centre_kernel(slots, lists, centroids, out):
    size = out.shape[0]
    first = pl.program_id(0) * size
    hit = slots[...] == iota((size, slots.shape[1]), 0) + first
    at = jnp.sum(jnp.where(hit, lists[...] + 1, 0), axis=1, keepdims=True) - 1
    onehot = (iota((size, centroids.shape[0]), 1) == at).astype(F32).astype(BF16)
    out[...] = jnp.dot(onehot, centroids[...], preferred_element_type=F32).astype(BF16)


def centres(slots, lists, centroids):
    count = slots.shape[1]
    n_lists, width = centroids.shape
    tile = fit(count, 256)
    return pl.pallas_call(
        centre_kernel,
        grid=(count // tile,),
        in_specs=[
            pl.BlockSpec((1, count), lambda i: (0, 0)),
            pl.BlockSpec((1, count), lambda i: (0, 0)),
            pl.BlockSpec((n_lists, width), lambda i: (0, 0)),
        ],
        out_specs=pl.BlockSpec((tile, width), lambda i: (i, 0)),
        out_shape=jax.ShapeDtypeStruct((count, width), BF16),
        compiler_params=params(48),
        cost_estimate=pl.CostEstimate(
            flops=2 * count * n_lists * width,
            bytes_accessed=2 * width * (count + n_lists),
            transcendentals=0,
        ),
        name="centroid_rows",
    )(slots, lists, centroids)


def place_kernel(slots, arrived, centre, out):
    size = out.shape[0]
    first = pl.program_id(0) * size
    onehot = (slots[...] == iota((size, slots.shape[1]), 0) + first).astype(F32).astype(BF16)
    keys = jnp.dot(onehot, arrived[...], preferred_element_type=F32)
    out[...] = (keys - centre[...].astype(F32)).astype(BF16)


def place_rows(slots, arrived, centre):
    count, width = centre.shape
    n_rows = arrived.shape[0]
    tile = fit(count, 256)
    return pl.pallas_call(
        place_kernel,
        grid=(count // tile,),
        in_specs=[
            pl.BlockSpec((1, n_rows), lambda i: (0, 0)),
            pl.BlockSpec((n_rows, width), lambda i: (0, 0)),
            pl.BlockSpec((tile, width), lambda i: (i, 0)),
        ],
        out_specs=pl.BlockSpec((tile, width), lambda i: (i, 0)),
        out_shape=jax.ShapeDtypeStruct((count, width), BF16),
        compiler_params=params(48),
        cost_estimate=pl.CostEstimate(
            flops=2 * count * n_rows * width,
            bytes_accessed=2 * width * (2 * count + n_rows),
            transcendentals=0,
        ),
        name="residual_rows",
    )(slots, arrived, centre)


def shards(hidden, norm_gain, projection, centroids, owners, local_list, slot_table):
    n_dp = lax.axis_size("dp")
    me = lax.axis_index("tp").astype(I32)
    rows = owners.shape[0]
    width = projection.shape[1]
    cap = slot_table.shape[1] // n_dp
    gain = norm_gain.reshape(1, -1)

    place, listed = route(owners.reshape(1, rows), local_list.reshape(1, rows), n_dp, cap)
    lists = lax.all_to_all(listed, "dp", split_axis=0, concat_axis=0, tiled=True)
    lists = lists[:, :cap].reshape(1, n_dp * cap)

    for_other = partial_keys((1 - me).reshape(1), hidden, gain, projection, rows)
    other = lax.ppermute(for_other, "tp", [(0, 1), (1, 0)])
    own = partial_keys(me.reshape(1), hidden, gain, projection, rows)
    outgoing = pack(own, other, place, n_dp * cap)
    arrived = lax.all_to_all(
        outgoing.reshape(n_dp, cap, width), "dp", split_axis=0, concat_axis=0, tiled=True
    ).reshape(n_dp * cap, width)

    centre = centres(slot_table, lists, centroids)
    live = jnp.where(lists >= 0, slot_table, -1)
    return place_rows(live, arrived, centre)


def solution(mesh):
    placed = (
        P("dp", "tp"),
        P("tp"),
        P("tp", None),
        P("dp", None),
        P(("dp", "tp"), None),
        P(("dp", "tp")),
        P(("dp", "tp"), None),
    )
    return jax.shard_map(
        shards, mesh=mesh, in_specs=placed, out_specs=P(("dp", "tp"), None), check_vma=False
    )
```

```python
import functools

import jax
import jax.numpy as jnp
from jax import lax
from jax.experimental import pallas as pl
from jax.experimental.pallas import tpu as pltpu
from jax.sharding import PartitionSpec as P

D = 8192
EPSILON = 1e-05
LANES = 128
MIB = 1024 * 1024
PLANES = 4
FAR_STRIDE = 4096
HIDDEN = pl.CostEstimate(flops=1, bytes_accessed=1, transcendentals=0)
F32 = jnp.float32
BF16 = jnp.bfloat16
I32 = jnp.int32


def iota(shape, dim):
    return lax.broadcasted_iota(I32, shape, dim)


def fit(total, wanted):
    best = 16
    for size in range(16, min(total, wanted) + 1, 16):
        if total % size == 0:
            best = size
    return best


def params(mib):
    return pltpu.CompilerParams(vmem_limit_bytes=mib * MIB)


def partial_kernel(which, hidden, gain, projection, out, total, squares):
    step = pl.program_id(0)
    rows, depth = hidden.shape
    tile = fit(rows, 512)

    @pl.when(step == 0)
    def _():
        total[...] = jnp.zeros_like(total)
        squares[...] = jnp.zeros_like(squares)

    @pl.loop(0, rows // tile)
    def _(i):
        at = pl.ds(pl.multiple_of(i * tile, tile), tile)
        block = hidden[at, :]
        total[at, :] += jnp.dot(block * gain[...], projection[...], preferred_element_type=F32)
        wide = block.astype(F32)
        wide = wide * wide
        part = wide[:, :LANES]
        for lane in range(LANES, depth, LANES):
            part = part + wide[:, lane : lane + LANES]
        squares[at, :] += part

    @pl.when(step == pl.num_programs(0) - 1)
    def _():
        width = total.shape[1]

        @pl.loop(0, rows // tile)
        def _(i):
            at = pl.ds(pl.multiple_of(i * tile, tile), tile)
            out[at, :width] = total[at, :].astype(BF16)
            energy = squares[at, :]
            high = energy.astype(BF16)
            wide = high.astype(F32)
            out[at, width : width + LANES] = high
            out[at, width + LANES :] = jnp.where(wide < 3e38, energy - wide, 0.0).astype(BF16)


def partial_keys(which, hidden, gain, projection, rows):
    depth, width = projection.shape
    block = 1024
    return pl.pallas_call(
        partial_kernel,
        grid_spec=pltpu.PrefetchScalarGridSpec(
            num_scalar_prefetch=1,
            grid=(depth // block,),
            in_specs=[
                pl.BlockSpec((rows, block), lambda k, w: (w[0], k)),
                pl.BlockSpec((1, block), lambda k, w: (0, k)),
                pl.BlockSpec((block, width), lambda k, w: (k, 0)),
            ],
            out_specs=pl.BlockSpec((rows, width + 2 * LANES), lambda k, w: (0, 0)),
            scratch_shapes=[pltpu.VMEM((rows, width), F32), pltpu.VMEM((rows, LANES), F32)],
        ),
        out_shape=jax.ShapeDtypeStruct((rows, width + 2 * LANES), BF16),
        compiler_params=params(60),
        cost_estimate=pl.CostEstimate(
            flops=2 * rows * depth * width,
            bytes_accessed=2 * (rows * depth + depth * width + rows * width),
            transcendentals=0,
        ),
        name="partial_keys",
    )(which, hidden, gain, projection)


def route_kernel(plan, me, owners, lists, place, sent):
    n_dp, cap = plan.n_dp, plan.cap
    size = plan.plane
    rows = owners.shape[1]
    n_own = plan.n_own
    wide = plan.wide
    plane = me[0] // size
    hot = iota((n_own, rows), 0) == owners[...]
    onehot = hot.astype(F32).astype(BF16)
    before = (iota((rows, rows), 0) < iota((rows, rows), 1)).astype(F32).astype(BF16)
    ranks = jnp.dot(onehot, before, preferred_element_type=F32)

    def of_token(column):
        return jnp.sum(jnp.where(hot, column, 0.0), axis=0, keepdims=True)

    def bits(owner):
        return jnp.where(owner < n_dp, (owner // size) ^ plane, PLANES)

    def counts(mask):
        return lax.dot_general(
            mask.astype(F32).astype(BF16), onehot, (((1,), (1,)), ((), ())), preferred_element_type=F32
        )[0:1, :]

    def column(mask):
        return jnp.sum(jnp.where(hot & mask, 1.0, 0.0), axis=1, keepdims=True)

    token = iota((1, rows), 1)
    early = token < plan.early
    direct_row = jnp.minimum(counts(iota((8, rows), 1) < plan.early), float(plan.direct))
    direct_col = jnp.minimum(column(early), float(plan.direct))
    all_row = counts(iota((8, rows), 1) >= 0) - direct_row
    all_col = column(token >= 0) - direct_col
    bits_row = bits(iota((1, n_own), 1))
    bits_col = bits(iota((n_own, 1), 0))

    level = iota((n_own, wide), 1).astype(F32)

    def wave(col, row, near_cap):
        out_col = jnp.where(bits_col == 0, jnp.minimum(col, near_cap), col)
        out_row = jnp.where(bits_row == 0, jnp.minimum(row, near_cap), row)
        for e in range(1, PLANES):
            mine = bits_col == e
            filled = jnp.sum(jnp.where(mine, jnp.minimum(col, level), 0.0), axis=0, keepdims=True)
            fits = (filled <= float(plan.far)) & (level[0:1, :] <= float(plan.each))
            limit = jnp.sum(jnp.where(fits, 1.0, 0.0), axis=1, keepdims=True) - 1.0
            out_col = jnp.where(mine, jnp.minimum(col, limit), out_col)
            out_row = jnp.where(bits_row == e, jnp.minimum(row, limit), out_row)
        return out_col, out_row

    half_col = jnp.where(bits_col == 0, all_col, jnp.floor((all_col + 1.0) * 0.5))
    half_row = jnp.where(bits_row == 0, all_row, jnp.floor((all_row + 1.0) * 0.5))
    first_col, first_row = wave(half_col, half_row, float(plan.near_cap))
    second_col, second_row = wave(all_col - first_col, all_row - first_row, 0.0)
    third_row = all_row - first_row - second_row

    def starts(row):
        ahead = (iota((n_own, n_own), 1) < iota((n_own, n_own), 0)) & (bits_row == bits_col)
        return jnp.sum(jnp.where(ahead, row, 0.0), axis=1, keepdims=True)

    by_rank = of_token(ranks)
    straight = early & (by_rank < of_token(direct_col))
    rank = by_rank - of_token(direct_col)
    first_n = of_token(first_col)
    second_n = of_token(second_col)
    e_token = (owners[...] // size) ^ plane
    in_first = ~straight & (rank < first_n)
    in_third = ~straight & (rank >= first_n + second_n)
    in_second = ~(straight | in_first | in_third)
    stride = (e_token - 1) * FAR_STRIDE
    first_at = stride + (of_token(starts(first_row)) + rank).astype(I32)
    second_at = stride + (of_token(starts(second_row)) + rank - first_n).astype(I32)
    third_at = owners[...] * cap + (rank - first_n - second_n).astype(I32)
    near_at = ((owners[...] % size) ^ (me[0] % size)) * plan.near_cap + rank.astype(I32)
    place[...] = jnp.full(place.shape, -1, I32)
    place[0:1, :] = jnp.where(in_first & (e_token > 0), first_at, -1)
    place[1:2, :] = jnp.where(in_first & (e_token == 0), near_at, -1)
    place[2:3, :] = jnp.where(in_second, second_at, -1)
    place[3:4, :] = jnp.where(straight, owners[...] * plan.direct + by_rank.astype(I32), -1)
    place[4:5, :] = jnp.where(in_third, third_at, -1)

    at_rank = (iota((wide, rows), 0).astype(F32) == by_rank).astype(F32).astype(BF16)
    high = (lists[...] // 64).astype(F32)
    low = (lists[...] % 64).astype(F32)

    def by_owner(values):
        picked = jnp.where(hot, values, 0.0).astype(BF16)
        return lax.dot_general(picked, at_rank, (((1,), (1,)), ((), ())), preferred_element_type=F32)

    live = by_owner(jnp.ones_like(high))
    ids = by_owner(high) * 64.0 + by_owner(low)
    step = jnp.max(third_row, axis=1, keepdims=True)
    for base in range(0, 2 * plan.sent, plan.sent):
        sent[:, base : base + wide] = jnp.where(live > 0.5, ids, -1.0).astype(I32)[:n_dp, :]
        start = base + wide
        for row in (direct_row, first_row, second_row):
            sent[:, start : start + n_own] = jnp.broadcast_to(row.astype(I32), (n_dp, n_own))
            start += n_own
        sent[:, start : start + LANES] = jnp.broadcast_to(step.astype(I32), (n_dp, LANES))


def route(plan, me, owners, lists):
    rows = owners.shape[1]
    return pl.pallas_call(
        functools.partial(route_kernel, plan),
        grid_spec=pltpu.PrefetchScalarGridSpec(
            num_scalar_prefetch=1,
            grid=(1,),
            in_specs=[pl.BlockSpec((1, rows), lambda i, m: (0, 0))] * 2,
            out_specs=(
                pl.BlockSpec((8, rows), lambda i, m: (0, 0)),
                pl.BlockSpec((plan.n_dp, 2 * plan.sent), lambda i, m: (0, 0)),
            ),
        ),
        out_shape=(
            jax.ShapeDtypeStruct((8, rows), I32),
            jax.ShapeDtypeStruct((plan.n_dp, 2 * plan.sent), I32),
        ),
        compiler_params=params(32),
        cost_estimate=pl.CostEstimate(
            flops=2 * rows * rows * plan.n_own, bytes_accessed=rows * 64, transcendentals=0
        ),
        name="route",
    )(me, owners, lists)


def slot_kernel(plan, me, heard, table, direct, near, first, second, third, counts):
    size = plan.plane
    wide, n_own = plan.wide, plan.n_own
    plane = me[0] // size
    owner = iota((plan.n_dp, n_own), 1)

    def listed(wave):
        return heard[:, wide + wave * n_own : wide + (wave + 1) * n_own]

    def mine(wave):
        return jnp.sum(jnp.where(owner == me[0], listed(wave), 0), axis=1, keepdims=True)

    def skip(slots, count):
        shift = 1
        while shift < wide:
            moved = pltpu.roll(slots, wide - shift, 1)
            slots = jnp.where((count // shift) % 2 == 1, moved, slots)
            shift *= 2
        return slots

    def of_bits(values, e):
        picked = jnp.zeros((size, values.shape[1]), I32)
        for q in range(PLANES):
            picked = jnp.where((plane ^ e) == q, values[q * size : (q + 1) * size, :], picked)
        return picked

    def by_distance(part, i):
        picked = iota((size, 1), 0) == ((me[0] % size) ^ i)
        return jnp.sum(jnp.where(picked, part, 0), axis=0, keepdims=True)

    n_direct, n_first, n_second = mine(0), mine(1), mine(2)
    total = jnp.sum(jnp.where(heard[:, :wide] >= 0, 1, 0), axis=1, keepdims=True)
    lane = iota((plan.n_dp, wide), 1)
    slots = table[...]
    direct[...] = jnp.where(lane < n_direct, slots, -1)
    slots = skip(slots, n_direct)
    in_first = jnp.where(lane < n_first, slots, -1)
    slots = skip(slots, n_first)
    in_second = jnp.where(lane < n_second, slots, -1)
    slots = skip(slots, n_second)
    third[...] = jnp.where(lane < total - n_direct - n_first - n_second, slots, -1)
    for i in range(size):
        near[i : i + 1, :] = by_distance(of_bits(in_first, 0), i)
    source = iota((plan.n_dp, 1), 0)
    for wave, values, out in ((0, in_first, first), (1, in_second, second)):
        for e in range(1, PLANES):
            part = of_bits(values, e)
            for i in range(size):
                at = i * (PLANES - 1) + e - 1
                out[at : at + 1, :] = by_distance(part, i)
            from_me = source == (plane ^ e) * size + me[0] % size
            at = wave * 4 + e - 1
            counts[at : at + 1, :] = jnp.sum(
                jnp.where(from_me, listed(1 + wave), 0), axis=0, keepdims=True
            )


def wave_slots(plan, me, heard, table):
    size = plan.plane
    shapes = [
        (plan.n_dp, plan.wide),
        (size, plan.wide),
        (size * (PLANES - 1), plan.wide),
        (size * (PLANES - 1), plan.wide),
        (plan.n_dp, plan.wide),
        (8, plan.n_own),
    ]
    return pl.pallas_call(
        functools.partial(slot_kernel, plan),
        grid_spec=pltpu.PrefetchScalarGridSpec(
            num_scalar_prefetch=1,
            grid=(1,),
            in_specs=[
                pl.BlockSpec((plan.n_dp, plan.sent), lambda i, m: (0, 0)),
                pl.BlockSpec((plan.n_dp, plan.wide), lambda i, m: (0, 0)),
            ],
            out_specs=tuple(pl.BlockSpec(shape, lambda i, m: (0, 0)) for shape in shapes),
        ),
        out_shape=tuple(jax.ShapeDtypeStruct(shape, I32) for shape in shapes),
        compiler_params=params(32),
        cost_estimate=HIDDEN,
        name="wave_slots",
    )(me, heard, table)


def combine(own, other, keys):
    rows, width = keys.shape
    tile = fit(rows, 128)

    @pl.loop(0, rows // tile)
    def _(i):
        at = pl.ds(pl.multiple_of(i * tile, tile), tile)
        parts = own[at, width:].astype(F32) + other[at, width:].astype(F32)
        energy = jnp.sum(parts, axis=1, keepdims=True)
        scale = lax.rsqrt(energy * (1.0 / D) + EPSILON)
        terms = own[at, :width].astype(F32) + other[at, :width].astype(F32)
        keys[at, :] = jnp.where(scale > 0.0, terms * scale, 0.0).astype(BF16)


def permute(line, first, place, chunks, out):
    total = None
    start = 0
    for keys in chunks:
        rows = keys.shape[0]
        places = place[line : line + 1, start : start + rows]
        start += rows
        onehot = (iota((out.shape[0], rows), 0) + first == places).astype(F32).astype(BF16)
        part = jnp.dot(onehot, keys[...], preferred_element_type=F32)
        total = part if total is None else total + part
    out[...] = total.astype(BF16)


def pack_kernel(moves, n_keys, fresh, place, *refs):
    chunks = refs[:n_keys]
    if fresh:
        own, other = refs[n_keys : n_keys + 2]
        outs, keys = refs[n_keys + 2 : -1], refs[-1]
        combine(own, other, keys)
        chunks = (*chunks, keys)
    else:
        outs = refs[n_keys:]
    for (line, first, _), out in zip(moves, outs):
        permute(line, first, place, chunks, out)


def pack(moves, place, keys, fresh=()):
    width = keys[0].shape[1] if keys else fresh[0].shape[1] - 2 * LANES
    sizes = [size for _, _, size in moves] + [part.shape[0] for part in fresh[:1]]
    rows = place.shape[1]
    whole = lambda i: (0, 0)
    operands = [place, *keys, *fresh]
    return list(
        pl.pallas_call(
            functools.partial(pack_kernel, moves, len(keys), bool(fresh)),
            grid=(1,),
            in_specs=[pl.BlockSpec(part.shape, whole) for part in operands],
            out_specs=tuple(pl.BlockSpec((size, width), whole) for size in sizes),
            out_shape=tuple(jax.ShapeDtypeStruct((size, width), BF16) for size in sizes),
            compiler_params=params(60),
            cost_estimate=HIDDEN,
            name="pack_keys",
        )(*operands)
    )


def spread_kernel(plan, wave, me, counts, *refs):
    size = plan.plane
    outs = refs[len(refs) - size :]
    refs = refs[: len(refs) - size]
    cap = plan.each
    base = (me[0] // size) * size
    for e in range(1, PLANES):
        rows = refs[e - 1]
        row = iota((cap, rows.shape[0]), 0)
        column = iota(row.shape, 1)
        at = wave * 4 + e - 1
        hits = []
        for k in range(size):
            owner = (me[0] % size) ^ k
            start = lax.fori_loop(0, owner, lambda i, total: total + counts[at, base + i], 0)
            hit = (column == row + start) & (row < counts[at, base + owner])
            hits.append(hit.astype(F32).astype(BF16))
        moved = jnp.dot(
            jnp.concatenate(hits, axis=0), rows[...], preferred_element_type=F32
        ).astype(BF16)
        for k in range(size):
            outs[k][(e - 1) * cap : e * cap, :] = moved[k * cap : (k + 1) * cap, :]


def spread(plan, wave, me, counts, packed):
    width = packed[0].shape[1]
    each = (PLANES - 1) * plan.each
    whole = lambda i, m, c: (0, 0)
    return list(
        pl.pallas_call(
            functools.partial(spread_kernel, plan, wave),
            grid_spec=pltpu.PrefetchScalarGridSpec(
                num_scalar_prefetch=2,
                grid=(1,),
                in_specs=[pl.BlockSpec(block.shape, whole) for block in packed],
                out_specs=(pl.BlockSpec((each, width), whole),) * plan.plane,
            ),
            out_shape=(jax.ShapeDtypeStruct((each, width), BF16),) * plan.plane,
            compiler_params=params(60),
            cost_estimate=HIDDEN,
            name="spread_rows",
        )(me, counts, *packed)
    )


def centre_kernel(n_in, slots, lists, centroids, out, table, placed):
    step = pl.program_id(0)
    block = centroids.shape[0]
    n_lists = n_in * block
    chunks = centroids.shape[1] // LANES
    count = placed.shape[0] // chunks
    size = out.shape[0]

    @pl.when(step == 0)
    def _():
        table[pl.ds(n_lists * chunks, chunks), :] = jnp.zeros((chunks, LANES), F32)

    @pl.when(step < n_in)
    def _():
        @pl.loop(0, block // 16)
        def _(i):
            wide = centroids[pl.ds(pl.multiple_of(i * 16, 16), 16), :].astype(F32)
            for top in range(0, 16, 8):
                first = (step * block + i * 16 + top) * chunks
                for c in range(chunks):
                    part = wide[top : top + 8, c * LANES : (c + 1) * LANES]
                    table[pl.ds(first + c, 8, stride=chunks), :] = part

    @pl.when(step == n_in)
    def _():
        @pl.loop(0, count // 16)
        def _(i):
            found = []
            for u in range(16):
                a = i * 16 + u
                row = table[pl.ds(pl.multiple_of(lists[a], chunks), chunks), :]
                found.append((slots[a], row))
            for at, row in found:
                placed[pl.ds(pl.multiple_of(at, chunks), chunks), :] = -row

    @pl.when(step >= n_in)
    def _():
        @pl.loop(0, size // 16)
        def _(i):
            rows = []
            for top in range(0, 16, 8):
                first = ((step - n_in) * size + i * 16 + top) * chunks
                rows.append(
                    jnp.concatenate(
                        [placed[pl.ds(first + c, 8, stride=chunks), :] for c in range(chunks)], axis=1
                    )
                )
            out[pl.ds(pl.multiple_of(i * 16, 16), 16), :] = jnp.concatenate(rows, axis=0).astype(BF16)


def centres(slots, lists, centroids):
    count = slots.shape[0]
    n_lists, width = centroids.shape
    slots = slots * (width // LANES)
    lists = jnp.where(lists < 0, n_lists, lists) * (width // LANES)
    block, size = fit(n_lists, 512), fit(count, 512)
    n_in = n_lists // block
    chunks = width // LANES
    return pl.pallas_call(
        functools.partial(centre_kernel, n_in),
        grid_spec=pltpu.PrefetchScalarGridSpec(
            num_scalar_prefetch=2,
            grid=(n_in + count // size,),
            in_specs=[pl.BlockSpec((block, width), lambda i, s, l: (jnp.minimum(i, n_in - 1), 0))],
            out_specs=pl.BlockSpec((size, width), lambda i, s, l: (jnp.maximum(i - n_in, 0), 0)),
            scratch_shapes=[
                pltpu.VMEM(((n_lists + 1) * chunks, LANES), F32),
                pltpu.VMEM((count * chunks, LANES), F32),
            ],
        ),
        out_shape=jax.ShapeDtypeStruct((count, width), BF16),
        compiler_params=params(60),
        cost_estimate=HIDDEN,
        name="centroid_rows",
    )(slots, lists, centroids)


def place_kernel(sizes, slots, before, *refs):
    parts, out, arrived, sems = refs[: len(sizes)], *refs[len(sizes) :]
    tile = out.shape[0]
    step = pl.program_id(0)
    first = step * tile

    @pl.when(step == 0)
    def _():
        copies = []
        start = 0
        for i, (part, size) in enumerate(zip(parts, sizes)):
            copies.append(pltpu.make_async_copy(part, arrived.at[pl.ds(start, size)], sems.at[i]))
            start += size
        for copy in copies:
            copy.start()
        for copy in copies:
            copy.wait()

    onehot = (slots[...] == iota((tile, slots.shape[1]), 0) + first).astype(F32).astype(BF16)
    keys = jnp.dot(onehot, arrived[...], preferred_element_type=F32)
    out[...] = (keys + before[...].astype(F32)).astype(BF16)


def place_rows(slots, arrived, before):
    count, width = before.shape
    sizes = [part.shape[0] for part in arrived]
    n_rows = sum(sizes)
    tile = fit(count, 512)
    return pl.pallas_call(
        functools.partial(place_kernel, sizes),
        grid=(count // tile,),
        in_specs=[
            pl.BlockSpec((1, n_rows), lambda i: (0, 0)),
            pl.BlockSpec((tile, width), lambda i: (i, 0)),
        ]
        + [pl.BlockSpec(memory_space=pl.ANY)] * len(sizes),
        out_specs=pl.BlockSpec((tile, width), lambda i: (i, 0)),
        out_shape=jax.ShapeDtypeStruct((count, width), BF16),
        scratch_shapes=[
            pltpu.VMEM((n_rows, width), BF16),
            pltpu.SemaphoreType.DMA((len(sizes),)),
        ],
        compiler_params=params(60),
        cost_estimate=HIDDEN,
        name="residual_rows",
    )(slots, before, *arrived)


def up16(value):
    return -(-value // 16) * 16


class Plan:
    def __init__(self, n_dp, rows, cap):
        self.n_dp, self.cap = n_dp, cap
        self.plane = n_dp // PLANES
        self.n_own = -(-n_dp // LANES) * LANES
        self.wide = -(-(cap + 1) // LANES) * LANES
        self.sent = self.wide + 3 * self.n_own + LANES
        self.early = rows // 2
        self.direct = up16(cap // 3)
        self.each = up16(cap // 3)
        self.near_cap = min(cap, up16(cap * 2 // 3))
        self.far = up16(rows * 9 // 64)


def shards(hidden, norm_gain, projection, centroids, owners, local_list, slot_table):
    n_dp = lax.axis_size("dp")
    me = lax.axis_index("tp").astype(I32)
    here = lax.axis_index("dp").astype(I32)
    rows = owners.shape[0]
    width = projection.shape[1]
    cap = slot_table.shape[1] // n_dp
    plan = Plan(n_dp, rows, cap)
    size = plan.plane
    gain = norm_gain.reshape(1, -1)
    groups = [list(range(q * size, (q + 1) * size)) for q in range(PLANES)]
    here = here.reshape(1)

    def across(blocks):
        pieces = len(blocks) // (PLANES - 1)
        return [
            lax.ppermute(
                block,
                "dp",
                [(p, ((p // size) ^ (1 + i // pieces)) * size + p % size) for p in range(n_dp)],
            )
            for i, block in enumerate(blocks)
        ]

    def exchange(blocks):
        return [blocks[0]] + [
            lax.ppermute(block, "dp", [(p, p - p % size + (p % size ^ k)) for p in range(n_dp)])
            for k, block in enumerate(blocks)
            if k > 0
        ]

    place, sent = route(plan, here, owners.reshape(1, rows), local_list.reshape(1, rows))
    heard = lax.all_to_all(
        sent.reshape(2 * n_dp, plan.sent), ("dp", "tp"), split_axis=0, concat_axis=0, tiled=True
    )
    def partials(chunk):
        half = rows // 2
        for_other = partial_keys((2 - 2 * me + chunk).reshape(1), hidden, gain, projection, half)
        other = lax.ppermute(for_other, "tp", [(0, 1), (1, 0)])
        own = partial_keys((2 * me + chunk).reshape(1), hidden, gain, projection, half)
        return own, other

    def direct(block):
        block = block.reshape(n_dp, -1, width)
        got = lax.all_to_all(block, "dp", split_axis=0, concat_axis=0, tiled=True)
        return got.reshape(-1, width)

    def fars(line):
        return [(line, e * FAR_STRIDE, plan.far) for e in range(PLANES - 1)]

    early_place = place[:, : plan.early]
    straight, early = pack([(3, 0, n_dp * plan.direct)], early_place, [], partials(0))
    straight = direct(straight)
    *far_first, late = pack(fars(0), place, [early], partials(1))
    far_first = across(far_first)
    nears = [(1, k * plan.near_cap, plan.near_cap) for k in range(size)]
    packed = pack(nears + fars(2), place, [early, late])
    near = exchange(packed[:size])
    far_second = across(packed[size:])

    level = jnp.max(heard[:, -1])
    heard = lax.dynamic_index_in_dim(heard.reshape(n_dp, 2, plan.sent), me, 1, keepdims=False)
    lists = heard[:, :cap].reshape(n_dp * cap)
    table = jnp.pad(slot_table.reshape(n_dp, cap), ((0, 0), (0, plan.wide - cap)))
    direct_slots, near_slots, first_slots, second_slots, third_slots, counts = wave_slots(
        plan, here, heard, table
    )
    centre = centres(slot_table.reshape(-1), lists, centroids)

    def flat(*parts):
        parts = [slots[:, :each].reshape(1, -1) for slots, each in parts]
        return jnp.concatenate(parts, axis=1) if len(parts) > 1 else parts[0]

    far_first, near, centre = lax.optimization_barrier((far_first, near, centre))
    passed = exchange(spread(plan, 0, here, counts, far_first))
    slots = flat((direct_slots, plan.direct), (near_slots, plan.near_cap))
    out = place_rows(slots, [straight, *near], centre)
    far_second, out = lax.optimization_barrier((far_second, out))
    blocks = spread(plan, 1, here, counts, far_second)
    blocks, passed = lax.optimization_barrier((blocks, passed))
    late_passed = exchange(blocks)
    slots = flat((first_slots, plan.each), (second_slots[: PLANES - 1], plan.each))
    out = place_rows(slots, [*passed, blocks[0]], out)
    slots = flat((second_slots[PLANES - 1 :], plan.each))

    def finish(args):
        return place_rows(args["slots"], args["rows"], args["out"])

    def finish_more(args):
        (more,) = pack([(4, 0, n_dp * cap)], args["place"], args["keys"])
        return place_rows(flat((args["third_slots"], cap)), [direct(more)], finish(args))

    return lax.cond(
        level > 0,
        finish_more,
        finish,
        dict(
            slots=slots, rows=late_passed[1:], out=out, place=place, keys=[early, late],
            third_slots=third_slots,
        ),
    )


def solution(mesh):
    placed = (
        P("dp", "tp"),
        P("tp"),
        P("tp", None),
        P("dp", None),
        P(("dp", "tp"), None),
        P(("dp", "tp")),
        P(("dp", "tp"), None),
    )
    return jax.shard_map(
        shards, mesh=mesh, in_specs=placed, out_specs=P(("dp", "tp"), None), check_vma=False
    )
```

```python
import functools

import jax
import jax.numpy as jnp
from jax import lax
from jax.experimental import pallas as pl
from jax.experimental.pallas import tpu as pltpu
from jax.sharding import PartitionSpec as P

D = 8192
EPSILON = 1e-05
LANES = 128
MIB = 1024 * 1024
PARTS = 2
F32 = jnp.float32
BF16 = jnp.bfloat16
I32 = jnp.int32


def iota(shape, dim):
    return lax.broadcasted_iota(I32, shape, dim)


def fit(total, wanted):
    best = 16
    for size in range(16, min(total, wanted) + 1, 16):
        if total % size == 0:
            best = size
    return best


def params(mib):
    return pltpu.CompilerParams(vmem_limit_bytes=mib * MIB)


def partial_kernel(which, hidden, gain, projection, out, total, squares):
    step = pl.program_id(0)
    rows, depth = hidden.shape
    tile = fit(rows, 1024)

    @pl.when(step == 0)
    def _():
        total[...] = jnp.zeros_like(total)
        squares[...] = jnp.zeros_like(squares)

    @pl.loop(0, rows // tile)
    def _(i):
        at = pl.ds(pl.multiple_of(i * tile, tile), tile)
        block = hidden[at, :]
        total[at, :] += jnp.dot(block * gain[...], projection[...], preferred_element_type=F32)
        wide = block.astype(F32)
        wide = wide * wide
        part = wide[:, :LANES]
        for lane in range(LANES, depth, LANES):
            part = part + wide[:, lane : lane + LANES]
        squares[at, :] += part

    @pl.when(step == pl.num_programs(0) - 1)
    def _():
        width = total.shape[1]

        @pl.loop(0, rows // tile)
        def _(i):
            at = pl.ds(pl.multiple_of(i * tile, tile), tile)
            out[at, :width] = total[at, :].astype(BF16)
            if out.shape[1] > width:
                energy = squares[at, :]
                high = energy.astype(BF16)
                wide = high.astype(F32)
                out[at, width : width + LANES] = high
                out[at, width + LANES :] = jnp.where(wide < 3e38, energy - wide, 0.0).astype(BF16)


def partial_keys(which, hidden, gain, projection, rows, part, parts):
    depth, width = projection.shape
    width = width // parts
    block = 1024
    wide = width + (2 * LANES if part == 0 else 0)
    return pl.pallas_call(
        partial_kernel,
        grid_spec=pltpu.PrefetchScalarGridSpec(
            num_scalar_prefetch=1,
            grid=(depth // block,),
            in_specs=[
                pl.BlockSpec((rows, block), lambda k, w: (w[0], k)),
                pl.BlockSpec((1, block), lambda k, w: (0, k)),
                pl.BlockSpec((block, width), lambda k, w: (k, part)),
            ],
            out_specs=pl.BlockSpec((rows, wide), lambda k, w: (0, 0)),
            scratch_shapes=[pltpu.VMEM((rows, width), F32), pltpu.VMEM((rows, LANES), F32)],
        ),
        out_shape=jax.ShapeDtypeStruct((rows, wide), BF16),
        compiler_params=params(60),
        cost_estimate=pl.CostEstimate(
            flops=2 * rows * depth * width,
            bytes_accessed=2 * (rows * depth + depth * width + rows * width),
            transcendentals=0,
        ),
        name="partial_keys",
    )(which, hidden, gain, projection)


def route_kernel(n_dp, cap, owners, lists, place, listed):
    rows = owners.shape[1]
    n_own = 128 if n_dp <= 128 else n_dp
    hot = iota((n_own, rows), 0) == owners[...]
    onehot = hot.astype(F32).astype(BF16)
    before = (iota((rows, rows), 0) < iota((rows, rows), 1)).astype(F32).astype(BF16)
    ranks = jnp.dot(onehot, before, preferred_element_type=F32)
    rank = jnp.sum(jnp.where(hot, ranks, 0.0), axis=0, keepdims=True).astype(I32)
    place[...] = jnp.broadcast_to(owners[...] * cap + rank, place.shape)
    at_rank = (iota((listed.shape[1], rows), 0) == rank).astype(F32).astype(BF16)
    high = (lists[...] // 64).astype(F32)
    low = (lists[...] % 64).astype(F32)

    def by_owner(values):
        picked = jnp.where(hot, values, 0.0).astype(BF16)
        return lax.dot_general(picked, at_rank, (((1,), (1,)), ((), ())), preferred_element_type=F32)

    live = by_owner(jnp.ones_like(high))
    ids = by_owner(high) * 64.0 + by_owner(low)
    found = jnp.where(live > 0.5, ids, -1.0).astype(I32)
    listed[...] = found[:n_dp, :]


def route(owners, lists, n_dp, cap):
    rows = owners.shape[1]
    wide = -(-cap // LANES) * LANES
    return pl.pallas_call(
        functools.partial(route_kernel, n_dp, cap),
        out_shape=(
            jax.ShapeDtypeStruct((8, rows), I32),
            jax.ShapeDtypeStruct((n_dp, wide), I32),
        ),
        compiler_params=params(32),
        cost_estimate=pl.CostEstimate(
            flops=2 * rows * rows * 128, bytes_accessed=rows * 64, transcendentals=0
        ),
        name="route",
    )(owners, lists)


def pack_kernel(own, other, own_first, other_first, place, out, keys):
    rows, width = keys.shape
    step = pl.program_id(0)

    @pl.when(step == 0)
    def _():
        tile = fit(rows, 128)

        @pl.loop(0, rows // tile)
        def _(i):
            at = pl.ds(pl.multiple_of(i * tile, tile), tile)
            parts = own_first[at, width:].astype(F32) + other_first[at, width:].astype(F32)
            energy = jnp.sum(parts, axis=1, keepdims=True)
            scale = lax.rsqrt(energy * (1.0 / D) + EPSILON)
            terms = own[at, :width].astype(F32) + other[at, :width].astype(F32)
            keys[at, :] = jnp.where(scale > 0.0, terms * scale, 0.0).astype(BF16)

    size = out.shape[0]
    onehot = (iota((size, rows), 0) + step * size == place[0:1, :]).astype(F32).astype(BF16)
    out[...] = jnp.dot(onehot, keys[...], preferred_element_type=F32).astype(BF16)


def pack(place, sums, first, total):
    rows = place.shape[1]
    width = first[0].shape[1] - 2 * LANES
    tile = fit(total, 768)
    whole = lambda i: (0, 0)
    operands = [*sums, *first, place]
    return pl.pallas_call(
        pack_kernel,
        grid=(total // tile,),
        in_specs=[pl.BlockSpec(part.shape, whole) for part in operands],
        out_specs=pl.BlockSpec((tile, width), lambda i: (i, 0)),
        out_shape=jax.ShapeDtypeStruct((total, width), BF16),
        scratch_shapes=[pltpu.VMEM((rows, width), BF16)],
        compiler_params=params(60),
        cost_estimate=pl.CostEstimate(
            flops=2 * total * rows * width,
            bytes_accessed=2 * width * (4 * rows + total),
            transcendentals=rows,
        ),
        name="pack_keys",
    )(*operands)


def centre_kernel(n_in, slots, lists, centroids, out, table, placed):
    step = pl.program_id(0)
    block = centroids.shape[0]
    n_lists = n_in * block
    chunks = centroids.shape[1] // LANES
    count = placed.shape[0] // chunks
    size = out.shape[0]

    @pl.when(step == 0)
    def _():
        table[pl.ds(n_lists * chunks, chunks), :] = jnp.zeros((chunks, LANES), F32)

    @pl.when(step < n_in)
    def _():
        @pl.loop(0, block // 16)
        def _(i):
            wide = centroids[pl.ds(pl.multiple_of(i * 16, 16), 16), :].astype(F32)
            for top in range(0, 16, 8):
                first = (step * block + i * 16 + top) * chunks
                for c in range(chunks):
                    part = wide[top : top + 8, c * LANES : (c + 1) * LANES]
                    table[pl.ds(first + c, 8, stride=chunks), :] = part

    @pl.when(step == n_in)
    def _():
        @pl.loop(0, count // 16)
        def _(i):
            found = []
            for u in range(16):
                a = i * 16 + u
                row = table[pl.ds(pl.multiple_of(lists[a], chunks), chunks), :]
                found.append((slots[a], row))
            for at, row in found:
                placed[pl.ds(pl.multiple_of(at, chunks), chunks), :] = -row

    @pl.when(step >= n_in)
    def _():
        @pl.loop(0, size // 16)
        def _(i):
            rows = []
            for top in range(0, 16, 8):
                first = ((step - n_in) * size + i * 16 + top) * chunks
                rows.append(
                    jnp.concatenate(
                        [placed[pl.ds(first + c, 8, stride=chunks), :] for c in range(chunks)], axis=1
                    )
                )
            out[pl.ds(pl.multiple_of(i * 16, 16), 16), :] = jnp.concatenate(rows, axis=0).astype(BF16)


def centres(slots, lists, centroids):
    count = slots.shape[0]
    n_lists, width = centroids.shape
    slots = slots * (width // LANES)
    lists = jnp.where(lists < 0, n_lists, lists) * (width // LANES)
    block, size = fit(n_lists, 512), fit(count, 512)
    n_in = n_lists // block
    chunks = width // LANES
    return pl.pallas_call(
        functools.partial(centre_kernel, n_in),
        grid_spec=pltpu.PrefetchScalarGridSpec(
            num_scalar_prefetch=2,
            grid=(n_in + count // size,),
            in_specs=[pl.BlockSpec((block, width), lambda i, s, l: (jnp.minimum(i, n_in - 1), 0))],
            out_specs=pl.BlockSpec((size, width), lambda i, s, l: (jnp.maximum(i - n_in, 0), 0)),
            scratch_shapes=[
                pltpu.VMEM(((n_lists + 1) * chunks, LANES), F32),
                pltpu.VMEM((count * chunks, LANES), F32),
            ],
        ),
        out_shape=jax.ShapeDtypeStruct((count, width), BF16),
        compiler_params=params(60),
        cost_estimate=pl.CostEstimate(
            flops=6400 * count * width, bytes_accessed=4 * count * width, transcendentals=0
        ),
        name="centroid_rows",
    )(slots, lists, centroids)


def place_kernel(slots, before, arrived, out):
    tile = out.shape[0]
    first = pl.program_id(0) * tile
    onehot = (slots[...] == iota((tile, slots.shape[1]), 0) + first).astype(F32).astype(BF16)
    keys = jnp.dot(onehot, arrived[...], preferred_element_type=F32)
    out[...] = (keys + before[...].astype(F32)).astype(BF16)


def place_rows(slots, arrived, before, part):
    count = before.shape[0]
    n_rows, width = arrived.shape
    tile = fit(count, 512)
    return pl.pallas_call(
        place_kernel,
        grid=(count // tile,),
        in_specs=[
            pl.BlockSpec((1, n_rows), lambda i: (0, 0)),
            pl.BlockSpec((tile, width), lambda i: (i, part)),
            pl.BlockSpec((n_rows, width), lambda i: (0, 0)),
        ],
        out_specs=pl.BlockSpec((tile, width), lambda i: (i, part)),
        out_shape=jax.ShapeDtypeStruct(before.shape, BF16),
        input_output_aliases={1: 0},
        compiler_params=params(60),
        cost_estimate=pl.CostEstimate(
            flops=2 * count * n_rows * width,
            bytes_accessed=2 * width * (2 * count + n_rows),
            transcendentals=0,
        ),
        name="residual_rows",
    )(slots, before, arrived)


def shards(hidden, norm_gain, projection, centroids, owners, local_list, slot_table):
    n_dp = lax.axis_size("dp")
    me = lax.axis_index("tp").astype(I32)
    rows = owners.shape[0]
    cap = slot_table.shape[1] // n_dp
    gain = norm_gain.reshape(1, -1)

    def exchange(block):
        block = block.reshape(n_dp, cap, -1)
        got = lax.all_to_all(block, "dp", split_axis=0, concat_axis=0, tiled=True)
        return got.reshape(n_dp * cap, -1)

    place, listed = route(owners.reshape(1, rows), local_list.reshape(1, rows), n_dp, cap)
    lists = lax.all_to_all(listed, "dp", split_axis=0, concat_axis=0, tiled=True)

    sums, arrived = [], []
    for part in range(PARTS):
        for_other = partial_keys((1 - me).reshape(1), hidden, gain, projection, rows, part, PARTS)
        other = lax.ppermute(for_other, "tp", [(0, 1), (1, 0)])
        own = partial_keys(me.reshape(1), hidden, gain, projection, rows, part, PARTS)
        sums.append((own, other))
        out = pack(place, sums[part], sums[0], n_dp * cap)
        if part == 0:
            out, lists = lax.optimization_barrier((out, lists))
        arrived.append(exchange(out))

    lists = lists[:, :cap].reshape(-1)
    total = centres(slot_table.reshape(-1), lists, centroids)
    slots = jnp.where(lists >= 0, slot_table.reshape(-1), -1).reshape(1, -1)
    for part in range(PARTS):
        total = place_rows(slots, arrived[part], total, part)
    return total


def solution(mesh):
    placed = (
        P("dp", "tp"),
        P("tp"),
        P("tp", None),
        P("dp", None),
        P(("dp", "tp"), None),
        P(("dp", "tp")),
        P(("dp", "tp"), None),
    )
    return jax.shard_map(
        shards, mesh=mesh, in_specs=placed, out_specs=P(("dp", "tp"), None), check_vma=False
    )
```

```python
import functools

import jax
import jax.numpy as jnp
from jax import lax
from jax.experimental import pallas as pl
from jax.experimental.pallas import tpu as pltpu
from jax.sharding import PartitionSpec as P

D = 8192
EPSILON = 1e-05
LANES = 128
MIB = 1024 * 1024
PLANES = 4
FAR_STRIDE = 4096
HIDDEN = pl.CostEstimate(flops=1, bytes_accessed=1, transcendentals=0)
F32 = jnp.float32
BF16 = jnp.bfloat16
I32 = jnp.int32


def iota(shape, dim):
    return lax.broadcasted_iota(I32, shape, dim)


def fit(total, wanted):
    best = 16
    for size in range(16, min(total, wanted) + 1, 16):
        if total % size == 0:
            best = size
    return best


def params(mib):
    return pltpu.CompilerParams(vmem_limit_bytes=mib * MIB)


def partial_kernel(which, hidden, gain, projection, out, total, squares):
    step = pl.program_id(0)
    rows, depth = hidden.shape
    tile = fit(rows, 512)

    @pl.when(step == 0)
    def _():
        total[...] = jnp.zeros_like(total)
        squares[...] = jnp.zeros_like(squares)

    @pl.loop(0, rows // tile)
    def _(i):
        at = pl.ds(pl.multiple_of(i * tile, tile), tile)
        block = hidden[at, :]
        total[at, :] += jnp.dot(block * gain[...], projection[...], preferred_element_type=F32)
        wide = block.astype(F32)
        wide = wide * wide
        part = wide[:, :LANES]
        for lane in range(LANES, depth, LANES):
            part = part + wide[:, lane : lane + LANES]
        squares[at, :] += part

    @pl.when(step == pl.num_programs(0) - 1)
    def _():
        width = total.shape[1]

        @pl.loop(0, rows // tile)
        def _(i):
            at = pl.ds(pl.multiple_of(i * tile, tile), tile)
            out[at, :width] = total[at, :].astype(BF16)
            energy = squares[at, :]
            high = energy.astype(BF16)
            wide = high.astype(F32)
            out[at, width : width + LANES] = high
            out[at, width + LANES :] = jnp.where(wide < 3e38, energy - wide, 0.0).astype(BF16)


def partial_keys(which, hidden, gain, projection, rows):
    depth, width = projection.shape
    block = 1024
    return pl.pallas_call(
        partial_kernel,
        grid_spec=pltpu.PrefetchScalarGridSpec(
            num_scalar_prefetch=1,
            grid=(depth // block,),
            in_specs=[
                pl.BlockSpec((rows, block), lambda k, w: (w[0], k)),
                pl.BlockSpec((1, block), lambda k, w: (0, k)),
                pl.BlockSpec((block, width), lambda k, w: (k, 0)),
            ],
            out_specs=pl.BlockSpec((rows, width + 2 * LANES), lambda k, w: (0, 0)),
            scratch_shapes=[pltpu.VMEM((rows, width), F32), pltpu.VMEM((rows, LANES), F32)],
        ),
        out_shape=jax.ShapeDtypeStruct((rows, width + 2 * LANES), BF16),
        compiler_params=params(60),
        cost_estimate=pl.CostEstimate(
            flops=2 * rows * depth * width,
            bytes_accessed=2 * (rows * depth + depth * width + rows * width),
            transcendentals=0,
        ),
        name="partial_keys",
    )(which, hidden, gain, projection)


def route_kernel(plan, me, owners, lists, place, sent):
    n_dp, cap = plan.n_dp, plan.cap
    size = plan.plane
    rows = owners.shape[1]
    n_own = plan.n_own
    wide = plan.wide
    plane = me[0] // size
    hot = iota((n_own, rows), 0) == owners[...]
    onehot = hot.astype(F32).astype(BF16)
    before = (iota((rows, rows), 0) < iota((rows, rows), 1)).astype(F32).astype(BF16)
    ranks = jnp.dot(onehot, before, preferred_element_type=F32)

    def of_token(column):
        return jnp.sum(jnp.where(hot, column, 0.0), axis=0, keepdims=True)

    def bits(owner):
        return jnp.where(owner < n_dp, (owner // size) ^ plane, PLANES)

    def counts(mask):
        return lax.dot_general(
            mask.astype(F32).astype(BF16), onehot, (((1,), (1,)), ((), ())), preferred_element_type=F32
        )[0:1, :]

    def column(mask):
        return jnp.sum(jnp.where(hot & mask, 1.0, 0.0), axis=1, keepdims=True)

    token = iota((1, rows), 1)
    early = token < plan.early
    direct_row = jnp.minimum(counts(iota((8, rows), 1) < plan.early), float(plan.direct))
    direct_col = jnp.minimum(column(early), float(plan.direct))
    all_row = counts(iota((8, rows), 1) >= 0) - direct_row
    all_col = column(token >= 0) - direct_col
    bits_row = bits(iota((1, n_own), 1))
    bits_col = bits(iota((n_own, 1), 0))

    level = iota((n_own, wide), 1).astype(F32)

    def wave(col, row, near_cap):
        out_col = jnp.where(bits_col == 0, jnp.minimum(col, near_cap), col)
        out_row = jnp.where(bits_row == 0, jnp.minimum(row, near_cap), row)
        for e in range(1, PLANES):
            mine = bits_col == e
            filled = jnp.sum(jnp.where(mine, jnp.minimum(col, level), 0.0), axis=0, keepdims=True)
            fits = (filled <= float(plan.far)) & (level[0:1, :] <= float(plan.each))
            limit = jnp.sum(jnp.where(fits, 1.0, 0.0), axis=1, keepdims=True) - 1.0
            out_col = jnp.where(mine, jnp.minimum(col, limit), out_col)
            out_row = jnp.where(bits_row == e, jnp.minimum(row, limit), out_row)
        return out_col, out_row

    half_col = jnp.where(bits_col == 0, all_col, jnp.floor((all_col + 1.0) * 0.5))
    half_row = jnp.where(bits_row == 0, all_row, jnp.floor((all_row + 1.0) * 0.5))
    first_col, first_row = wave(half_col, half_row, float(plan.near_cap))
    second_col, second_row = wave(all_col - first_col, all_row - first_row, 0.0)
    third_row = all_row - first_row - second_row

    def starts(row):
        ahead = (iota((n_own, n_own), 1) < iota((n_own, n_own), 0)) & (bits_row == bits_col)
        return jnp.sum(jnp.where(ahead, row, 0.0), axis=1, keepdims=True)

    by_rank = of_token(ranks)
    straight = early & (by_rank < of_token(direct_col))
    rank = by_rank - of_token(direct_col)
    first_n = of_token(first_col)
    second_n = of_token(second_col)
    e_token = (owners[...] // size) ^ plane
    in_first = ~straight & (rank < first_n)
    in_third = ~straight & (rank >= first_n + second_n)
    in_second = ~(straight | in_first | in_third)
    stride = (e_token - 1) * FAR_STRIDE
    first_at = stride + (of_token(starts(first_row)) + rank).astype(I32)
    second_at = stride + (of_token(starts(second_row)) + rank - first_n).astype(I32)
    third_at = owners[...] * cap + (rank - first_n - second_n).astype(I32)
    near_at = ((owners[...] % size) ^ (me[0] % size)) * plan.near_cap + rank.astype(I32)
    place[...] = jnp.full(place.shape, -1, I32)
    place[0:1, :] = jnp.where(in_first & (e_token > 0), first_at, -1)
    place[1:2, :] = jnp.where(in_first & (e_token == 0), near_at, -1)
    place[2:3, :] = jnp.where(in_second, second_at, -1)
    place[3:4, :] = jnp.where(straight, owners[...] * plan.direct + by_rank.astype(I32), -1)
    place[4:5, :] = jnp.where(in_third, third_at, -1)

    at_rank = (iota((wide, rows), 0).astype(F32) == by_rank).astype(F32).astype(BF16)
    high = (lists[...] // 64).astype(F32)
    low = (lists[...] % 64).astype(F32)

    def by_owner(values):
        picked = jnp.where(hot, values, 0.0).astype(BF16)
        return lax.dot_general(picked, at_rank, (((1,), (1,)), ((), ())), preferred_element_type=F32)

    live = by_owner(jnp.ones_like(high))
    ids = by_owner(high) * 64.0 + by_owner(low)
    step = jnp.max(third_row, axis=1, keepdims=True)
    for base in range(0, 2 * plan.sent, plan.sent):
        sent[:, base : base + wide] = jnp.where(live > 0.5, ids, -1.0).astype(I32)[:n_dp, :]
        start = base + wide
        for row in (direct_row, first_row, second_row):
            sent[:, start : start + n_own] = jnp.broadcast_to(row.astype(I32), (n_dp, n_own))
            start += n_own
        sent[:, start : start + LANES] = jnp.broadcast_to(step.astype(I32), (n_dp, LANES))


def route(plan, me, owners, lists):
    rows = owners.shape[1]
    return pl.pallas_call(
        functools.partial(route_kernel, plan),
        grid_spec=pltpu.PrefetchScalarGridSpec(
            num_scalar_prefetch=1,
            grid=(1,),
            in_specs=[pl.BlockSpec((1, rows), lambda i, m: (0, 0))] * 2,
            out_specs=(
                pl.BlockSpec((8, rows), lambda i, m: (0, 0)),
                pl.BlockSpec((plan.n_dp, 2 * plan.sent), lambda i, m: (0, 0)),
            ),
        ),
        out_shape=(
            jax.ShapeDtypeStruct((8, rows), I32),
            jax.ShapeDtypeStruct((plan.n_dp, 2 * plan.sent), I32),
        ),
        compiler_params=params(32),
        cost_estimate=pl.CostEstimate(
            flops=2 * rows * rows * plan.n_own, bytes_accessed=rows * 64, transcendentals=0
        ),
        name="route",
    )(me, owners, lists)


def slot_kernel(plan, me, heard, table, direct, near, first, second, third, counts):
    size = plan.plane
    wide, n_own = plan.wide, plan.n_own
    plane = me[0] // size
    owner = iota((plan.n_dp, n_own), 1)

    def listed(wave):
        return heard[:, wide + wave * n_own : wide + (wave + 1) * n_own]

    def mine(wave):
        return jnp.sum(jnp.where(owner == me[0], listed(wave), 0), axis=1, keepdims=True)

    def skip(slots, count):
        shift = 1
        while shift < wide:
            moved = pltpu.roll(slots, wide - shift, 1)
            slots = jnp.where((count // shift) % 2 == 1, moved, slots)
            shift *= 2
        return slots

    def of_bits(values, e):
        picked = jnp.zeros((size, values.shape[1]), I32)
        for q in range(PLANES):
            picked = jnp.where((plane ^ e) == q, values[q * size : (q + 1) * size, :], picked)
        return picked

    def by_distance(part, i):
        picked = iota((size, 1), 0) == ((me[0] % size) ^ i)
        return jnp.sum(jnp.where(picked, part, 0), axis=0, keepdims=True)

    n_direct, n_first, n_second = mine(0), mine(1), mine(2)
    total = jnp.sum(jnp.where(heard[:, :wide] >= 0, 1, 0), axis=1, keepdims=True)
    lane = iota((plan.n_dp, wide), 1)
    slots = table[...]
    direct[...] = jnp.where(lane < n_direct, slots, -1)
    slots = skip(slots, n_direct)
    in_first = jnp.where(lane < n_first, slots, -1)
    slots = skip(slots, n_first)
    in_second = jnp.where(lane < n_second, slots, -1)
    slots = skip(slots, n_second)
    third[...] = jnp.where(lane < total - n_direct - n_first - n_second, slots, -1)
    for i in range(size):
        near[i : i + 1, :] = by_distance(of_bits(in_first, 0), i)
    source = iota((plan.n_dp, 1), 0)
    for wave, values, out in ((0, in_first, first), (1, in_second, second)):
        for e in range(1, PLANES):
            part = of_bits(values, e)
            for i in range(size):
                at = i * (PLANES - 1) + e - 1
                out[at : at + 1, :] = by_distance(part, i)
            from_me = source == (plane ^ e) * size + me[0] % size
            at = wave * 4 + e - 1
            counts[at : at + 1, :] = jnp.sum(
                jnp.where(from_me, listed(1 + wave), 0), axis=0, keepdims=True
            )


def wave_slots(plan, me, heard, table):
    size = plan.plane
    shapes = [
        (plan.n_dp, plan.wide),
        (size, plan.wide),
        (size * (PLANES - 1), plan.wide),
        (size * (PLANES - 1), plan.wide),
        (plan.n_dp, plan.wide),
        (8, plan.n_own),
    ]
    return pl.pallas_call(
        functools.partial(slot_kernel, plan),
        grid_spec=pltpu.PrefetchScalarGridSpec(
            num_scalar_prefetch=1,
            grid=(1,),
            in_specs=[
                pl.BlockSpec((plan.n_dp, plan.sent), lambda i, m: (0, 0)),
                pl.BlockSpec((plan.n_dp, plan.wide), lambda i, m: (0, 0)),
            ],
            out_specs=tuple(pl.BlockSpec(shape, lambda i, m: (0, 0)) for shape in shapes),
        ),
        out_shape=tuple(jax.ShapeDtypeStruct(shape, I32) for shape in shapes),
        compiler_params=params(32),
        cost_estimate=HIDDEN,
        name="wave_slots",
    )(me, heard, table)


def combine(own, other, keys):
    rows, width = keys.shape
    tile = fit(rows, 128)

    @pl.loop(0, rows // tile)
    def _(i):
        at = pl.ds(pl.multiple_of(i * tile, tile), tile)
        parts = own[at, width:].astype(F32) + other[at, width:].astype(F32)
        energy = jnp.sum(parts, axis=1, keepdims=True)
        scale = lax.rsqrt(energy * (1.0 / D) + EPSILON)
        terms = own[at, :width].astype(F32) + other[at, :width].astype(F32)
        keys[at, :] = jnp.where(scale > 0.0, terms * scale, 0.0).astype(BF16)


def permute(line, first, place, chunks, out):
    total = None
    start = 0
    for keys in chunks:
        rows = keys.shape[0]
        places = place[line : line + 1, start : start + rows]
        start += rows
        onehot = (iota((out.shape[0], rows), 0) + first == places).astype(F32).astype(BF16)
        part = jnp.dot(onehot, keys[...], preferred_element_type=F32)
        total = part if total is None else total + part
    out[...] = total.astype(BF16)


def pack_kernel(moves, n_keys, fresh, place, *refs):
    chunks = refs[:n_keys]
    if fresh:
        own, other = refs[n_keys : n_keys + 2]
        outs, keys = refs[n_keys + 2 : -1], refs[-1]
        combine(own, other, keys)
        chunks = (*chunks, keys)
    else:
        outs = refs[n_keys:]
    for (line, first, _), out in zip(moves, outs):
        permute(line, first, place, chunks, out)


def pack(moves, place, keys, fresh=()):
    width = keys[0].shape[1] if keys else fresh[0].shape[1] - 2 * LANES
    sizes = [size for _, _, size in moves] + [part.shape[0] for part in fresh[:1]]
    rows = place.shape[1]
    whole = lambda i: (0, 0)
    operands = [place, *keys, *fresh]
    return list(
        pl.pallas_call(
            functools.partial(pack_kernel, moves, len(keys), bool(fresh)),
            grid=(1,),
            in_specs=[pl.BlockSpec(part.shape, whole) for part in operands],
            out_specs=tuple(pl.BlockSpec((size, width), whole) for size in sizes),
            out_shape=tuple(jax.ShapeDtypeStruct((size, width), BF16) for size in sizes),
            compiler_params=params(60),
            cost_estimate=HIDDEN,
            name="pack_keys",
        )(*operands)
    )


def spread_kernel(plan, wave, me, counts, *refs):
    size = plan.plane
    outs = refs[len(refs) - size :]
    refs = refs[: len(refs) - size]
    cap = plan.each
    base = (me[0] // size) * size
    for e in range(1, PLANES):
        rows = refs[e - 1]
        row = iota((cap, rows.shape[0]), 0)
        column = iota(row.shape, 1)
        at = wave * 4 + e - 1
        hits = []
        for k in range(size):
            owner = (me[0] % size) ^ k
            start = lax.fori_loop(0, owner, lambda i, total: total + counts[at, base + i], 0)
            hit = (column == row + start) & (row < counts[at, base + owner])
            hits.append(hit.astype(F32).astype(BF16))
        moved = jnp.dot(
            jnp.concatenate(hits, axis=0), rows[...], preferred_element_type=F32
        ).astype(BF16)
        for k in range(size):
            outs[k][(e - 1) * cap : e * cap, :] = moved[k * cap : (k + 1) * cap, :]


def spread(plan, wave, me, counts, packed):
    width = packed[0].shape[1]
    each = (PLANES - 1) * plan.each
    whole = lambda i, m, c: (0, 0)
    return list(
        pl.pallas_call(
            functools.partial(spread_kernel, plan, wave),
            grid_spec=pltpu.PrefetchScalarGridSpec(
                num_scalar_prefetch=2,
                grid=(1,),
                in_specs=[pl.BlockSpec(block.shape, whole) for block in packed],
                out_specs=(pl.BlockSpec((each, width), whole),) * plan.plane,
            ),
            out_shape=(jax.ShapeDtypeStruct((each, width), BF16),) * plan.plane,
            compiler_params=params(60),
            cost_estimate=HIDDEN,
            name="spread_rows",
        )(me, counts, *packed)
    )


def centre_kernel(n_in, slots, lists, centroids, out, table, placed):
    step = pl.program_id(0)
    block = centroids.shape[0]
    n_lists = n_in * block
    chunks = centroids.shape[1] // LANES
    count = placed.shape[0] // chunks
    size = out.shape[0]

    @pl.when(step == 0)
    def _():
        table[pl.ds(n_lists * chunks, chunks), :] = jnp.zeros((chunks, LANES), F32)

    @pl.when(step < n_in)
    def _():
        @pl.loop(0, block // 16)
        def _(i):
            wide = centroids[pl.ds(pl.multiple_of(i * 16, 16), 16), :].astype(F32)
            for top in range(0, 16, 8):
                first = (step * block + i * 16 + top) * chunks
                for c in range(chunks):
                    part = wide[top : top + 8, c * LANES : (c + 1) * LANES]
                    table[pl.ds(first + c, 8, stride=chunks), :] = part

    @pl.when(step == n_in)
    def _():
        @pl.loop(0, count // 16)
        def _(i):
            found = []
            for u in range(16):
                a = i * 16 + u
                row = table[pl.ds(pl.multiple_of(lists[a], chunks), chunks), :]
                found.append((slots[a], row))
            for at, row in found:
                placed[pl.ds(pl.multiple_of(at, chunks), chunks), :] = -row

    @pl.when(step >= n_in)
    def _():
        @pl.loop(0, size // 16)
        def _(i):
            rows = []
            for top in range(0, 16, 8):
                first = ((step - n_in) * size + i * 16 + top) * chunks
                rows.append(
                    jnp.concatenate(
                        [placed[pl.ds(first + c, 8, stride=chunks), :] for c in range(chunks)], axis=1
                    )
                )
            out[pl.ds(pl.multiple_of(i * 16, 16), 16), :] = jnp.concatenate(rows, axis=0).astype(BF16)


def centres(slots, lists, centroids):
    count = slots.shape[0]
    n_lists, width = centroids.shape
    slots = slots * (width // LANES)
    lists = jnp.where(lists < 0, n_lists, lists) * (width // LANES)
    block, size = fit(n_lists, 512), fit(count, 512)
    n_in = n_lists // block
    chunks = width // LANES
    return pl.pallas_call(
        functools.partial(centre_kernel, n_in),
        grid_spec=pltpu.PrefetchScalarGridSpec(
            num_scalar_prefetch=2,
            grid=(n_in + count // size,),
            in_specs=[pl.BlockSpec((block, width), lambda i, s, l: (jnp.minimum(i, n_in - 1), 0))],
            out_specs=pl.BlockSpec((size, width), lambda i, s, l: (jnp.maximum(i - n_in, 0), 0)),
            scratch_shapes=[
                pltpu.VMEM(((n_lists + 1) * chunks, LANES), F32),
                pltpu.VMEM((count * chunks, LANES), F32),
            ],
        ),
        out_shape=jax.ShapeDtypeStruct((count, width), BF16),
        compiler_params=params(60),
        cost_estimate=HIDDEN,
        name="centroid_rows",
    )(slots, lists, centroids)


def place_kernel(sizes, slots, before, *refs):
    parts, out, arrived, sems = refs[: len(sizes)], *refs[len(sizes) :]
    tile = out.shape[0]
    step = pl.program_id(0)
    first = step * tile

    @pl.when(step == 0)
    def _():
        copies = []
        start = 0
        for i, (part, size) in enumerate(zip(parts, sizes)):
            copies.append(pltpu.make_async_copy(part, arrived.at[pl.ds(start, size)], sems.at[i]))
            start += size
        for copy in copies:
            copy.start()
        for copy in copies:
            copy.wait()

    onehot = (slots[...] == iota((tile, slots.shape[1]), 0) + first).astype(F32).astype(BF16)
    keys = jnp.dot(onehot, arrived[...], preferred_element_type=F32)
    out[...] = (keys + before[...].astype(F32)).astype(BF16)


def place_rows(slots, arrived, before):
    count, width = before.shape
    sizes = [part.shape[0] for part in arrived]
    n_rows = sum(sizes)
    tile = fit(count, 512)
    return pl.pallas_call(
        functools.partial(place_kernel, sizes),
        grid=(count // tile,),
        in_specs=[
            pl.BlockSpec((1, n_rows), lambda i: (0, 0)),
            pl.BlockSpec((tile, width), lambda i: (i, 0)),
        ]
        + [pl.BlockSpec(memory_space=pl.ANY)] * len(sizes),
        out_specs=pl.BlockSpec((tile, width), lambda i: (i, 0)),
        out_shape=jax.ShapeDtypeStruct((count, width), BF16),
        scratch_shapes=[
            pltpu.VMEM((n_rows, width), BF16),
            pltpu.SemaphoreType.DMA((len(sizes),)),
        ],
        compiler_params=params(60),
        cost_estimate=HIDDEN,
        name="residual_rows",
    )(slots, before, *arrived)


def up16(value):
    return -(-value // 16) * 16


class Plan:
    def __init__(self, n_dp, rows, cap):
        self.n_dp, self.cap = n_dp, cap
        self.plane = n_dp // PLANES
        self.n_own = -(-n_dp // LANES) * LANES
        self.wide = -(-(cap + 1) // LANES) * LANES
        self.sent = self.wide + 3 * self.n_own + LANES
        self.early = rows // 2
        self.direct = up16(cap // 3)
        self.each = up16(cap // 3)
        self.near_cap = min(cap, up16(cap * 2 // 3))
        self.far = up16(rows * 11 // 64)


def shards(hidden, norm_gain, projection, centroids, owners, local_list, slot_table):
    n_dp = lax.axis_size("dp")
    me = lax.axis_index("tp").astype(I32)
    here = lax.axis_index("dp").astype(I32)
    rows = owners.shape[0]
    width = projection.shape[1]
    cap = slot_table.shape[1] // n_dp
    plan = Plan(n_dp, rows, cap)
    size = plan.plane
    gain = norm_gain.reshape(1, -1)
    groups = [list(range(q * size, (q + 1) * size)) for q in range(PLANES)]
    here = here.reshape(1)

    def across(blocks):
        pieces = len(blocks) // (PLANES - 1)
        return [
            lax.ppermute(
                block,
                "dp",
                [(p, ((p // size) ^ (1 + i // pieces)) * size + p % size) for p in range(n_dp)],
            )
            for i, block in enumerate(blocks)
        ]

    def exchange(blocks):
        return [blocks[0]] + [
            lax.ppermute(block, "dp", [(p, p - p % size + (p % size ^ k)) for p in range(n_dp)])
            for k, block in enumerate(blocks)
            if k > 0
        ]

    place, sent = route(plan, here, owners.reshape(1, rows), local_list.reshape(1, rows))
    heard = lax.all_to_all(
        sent.reshape(2 * n_dp, plan.sent), ("dp", "tp"), split_axis=0, concat_axis=0, tiled=True
    )
    def partials(chunk):
        half = rows // 2
        for_other = partial_keys((2 - 2 * me + chunk).reshape(1), hidden, gain, projection, half)
        other = lax.ppermute(for_other, "tp", [(0, 1), (1, 0)])
        own = partial_keys((2 * me + chunk).reshape(1), hidden, gain, projection, half)
        return own, other

    def direct(block):
        block = block.reshape(n_dp, -1, width)
        got = lax.all_to_all(block, "dp", split_axis=0, concat_axis=0, tiled=True)
        return got.reshape(-1, width)

    def fars(line):
        return [(line, e * FAR_STRIDE, plan.far) for e in range(PLANES - 1)]

    early_place = place[:, : plan.early]
    straight, early = pack([(3, 0, n_dp * plan.direct)], early_place, [], partials(0))
    straight = direct(straight)
    *far_first, late = pack(fars(0), place, [early], partials(1))
    far_first = across(far_first)
    nears = [(1, k * plan.near_cap, plan.near_cap) for k in range(size)]
    packed = pack(nears + fars(2), place, [early, late])
    near = exchange(packed[:size])
    far_second = across(packed[size:])

    level = jnp.max(heard[:, -1])
    heard = lax.dynamic_index_in_dim(heard.reshape(n_dp, 2, plan.sent), me, 1, keepdims=False)
    lists = heard[:, :cap].reshape(n_dp * cap)
    table = jnp.pad(slot_table.reshape(n_dp, cap), ((0, 0), (0, plan.wide - cap)))
    direct_slots, near_slots, first_slots, second_slots, third_slots, counts = wave_slots(
        plan, here, heard, table
    )
    centre = centres(slot_table.reshape(-1), lists, centroids)

    def flat(*parts):
        parts = [slots[:, :each].reshape(1, -1) for slots, each in parts]
        return jnp.concatenate(parts, axis=1) if len(parts) > 1 else parts[0]

    far_first, near, centre = lax.optimization_barrier((far_first, near, centre))
    passed = exchange(spread(plan, 0, here, counts, far_first))
    slots = flat((direct_slots, plan.direct), (near_slots, plan.near_cap))
    out = place_rows(slots, [straight, *near], centre)
    far_second, out = lax.optimization_barrier((far_second, out))
    blocks = spread(plan, 1, here, counts, far_second)
    blocks, passed = lax.optimization_barrier((blocks, passed))
    late_passed = exchange(blocks)
    slots = flat((first_slots, plan.each), (second_slots[: PLANES - 1], plan.each))
    out = place_rows(slots, [*passed, blocks[0]], out)
    slots = flat((second_slots[PLANES - 1 :], plan.each))

    def finish(args):
        return place_rows(args["slots"], args["rows"], args["out"])

    def finish_more(size):
        def branch(args):
            third = args["place"][4:5]
            third = jnp.where(third < 0, -1, third // cap * size + third % cap)
            third = jnp.broadcast_to(third, args["place"].shape)
            (more,) = pack([(0, 0, n_dp * size)], third, args["keys"])
            return place_rows(flat((args["third_slots"], size)), [direct(more)], finish(args))

        return branch

    few = up16(cap // 3)
    return lax.switch(
        (level > 0).astype(I32) + (level > few).astype(I32),
        [finish, finish_more(few), finish_more(cap)],
        dict(
            slots=slots, rows=late_passed[1:], out=out, place=place, keys=[early, late],
            third_slots=third_slots,
        ),
    )


def solution(mesh):
    placed = (
        P("dp", "tp"),
        P("tp"),
        P("tp", None),
        P("dp", None),
        P(("dp", "tp"), None),
        P(("dp", "tp")),
        P(("dp", "tp"), None),
    )
    return jax.shard_map(
        shards, mesh=mesh, in_specs=placed, out_specs=P(("dp", "tp"), None), check_vma=False
    )
```

```python
import functools

import jax
import jax.numpy as jnp
from jax import lax
from jax.experimental import pallas as pl
from jax.experimental.pallas import tpu as pltpu
from jax.sharding import PartitionSpec as P

D = 8192
EPSILON = 1e-05
LANES = 128
MIB = 1024 * 1024
PLANES = 4
FAR_STRIDE = 4096
HIDDEN = pl.CostEstimate(flops=1, bytes_accessed=1, transcendentals=0)
F32 = jnp.float32
BF16 = jnp.bfloat16
I32 = jnp.int32


def iota(shape, dim):
    return lax.broadcasted_iota(I32, shape, dim)


def fit(total, wanted):
    best = 16
    for size in range(16, min(total, wanted) + 1, 16):
        if total % size == 0:
            best = size
    return best


def params(mib):
    return pltpu.CompilerParams(vmem_limit_bytes=mib * MIB)


def partial_kernel(which, hidden, gain, projection, out, total, squares):
    step = pl.program_id(0)
    rows, depth = hidden.shape
    tile = fit(rows, 512)

    @pl.when(step == 0)
    def _():
        total[...] = jnp.zeros_like(total)
        squares[...] = jnp.zeros_like(squares)

    @pl.loop(0, rows // tile)
    def _(i):
        at = pl.ds(pl.multiple_of(i * tile, tile), tile)
        block = hidden[at, :]
        total[at, :] += jnp.dot(block * gain[...], projection[...], preferred_element_type=F32)
        wide = block.astype(F32)
        wide = wide * wide
        part = wide[:, :LANES]
        for lane in range(LANES, depth, LANES):
            part = part + wide[:, lane : lane + LANES]
        squares[at, :] += part

    @pl.when(step == pl.num_programs(0) - 1)
    def _():
        width = total.shape[1]

        @pl.loop(0, rows // tile)
        def _(i):
            at = pl.ds(pl.multiple_of(i * tile, tile), tile)
            out[at, :width] = total[at, :].astype(BF16)
            energy = squares[at, :]
            high = energy.astype(BF16)
            wide = high.astype(F32)
            out[at, width : width + LANES] = high
            out[at, width + LANES :] = jnp.where(wide < 3e38, energy - wide, 0.0).astype(BF16)


def partial_keys(which, hidden, gain, projection, rows):
    depth, width = projection.shape
    block = 1024
    return pl.pallas_call(
        partial_kernel,
        grid_spec=pltpu.PrefetchScalarGridSpec(
            num_scalar_prefetch=1,
            grid=(depth // block,),
            in_specs=[
                pl.BlockSpec((rows, block), lambda k, w: (w[0], k)),
                pl.BlockSpec((1, block), lambda k, w: (0, k)),
                pl.BlockSpec((block, width), lambda k, w: (k, 0)),
            ],
            out_specs=pl.BlockSpec((rows, width + 2 * LANES), lambda k, w: (0, 0)),
            scratch_shapes=[pltpu.VMEM((rows, width), F32), pltpu.VMEM((rows, LANES), F32)],
        ),
        out_shape=jax.ShapeDtypeStruct((rows, width + 2 * LANES), BF16),
        compiler_params=params(60),
        cost_estimate=pl.CostEstimate(
            flops=2 * rows * depth * width,
            bytes_accessed=2 * (rows * depth + depth * width + rows * width),
            transcendentals=0,
        ),
        name="partial_keys",
    )(which, hidden, gain, projection)


def route_kernel(plan, me, owners, lists, place, sent):
    n_dp, cap = plan.n_dp, plan.cap
    size = plan.plane
    rows = owners.shape[1]
    n_own = plan.n_own
    wide = plan.wide
    plane = me[0] // size
    hot = iota((n_own, rows), 0) == owners[...]
    onehot = hot.astype(F32).astype(BF16)
    before = (iota((rows, rows), 0) < iota((rows, rows), 1)).astype(F32).astype(BF16)
    ranks = jnp.dot(onehot, before, preferred_element_type=F32)

    def of_token(column):
        return jnp.sum(jnp.where(hot, column, 0.0), axis=0, keepdims=True)

    def bits(owner):
        return jnp.where(owner < n_dp, (owner // size) ^ plane, PLANES)

    def counts(mask):
        return lax.dot_general(
            mask.astype(F32).astype(BF16), onehot, (((1,), (1,)), ((), ())), preferred_element_type=F32
        )[0:1, :]

    def column(mask):
        return jnp.sum(jnp.where(hot & mask, 1.0, 0.0), axis=1, keepdims=True)

    token = iota((1, rows), 1)
    early = token < plan.early
    direct_row = jnp.minimum(counts(iota((8, rows), 1) < plan.early), float(plan.direct))
    direct_col = jnp.minimum(column(early), float(plan.direct))
    all_row = counts(iota((8, rows), 1) >= 0) - direct_row
    all_col = column(token >= 0) - direct_col
    bits_row = bits(iota((1, n_own), 1))
    bits_col = bits(iota((n_own, 1), 0))

    level = iota((n_own, wide), 1).astype(F32)

    def wave(col, row, near_cap):
        out_col = jnp.where(bits_col == 0, jnp.minimum(col, near_cap), col)
        out_row = jnp.where(bits_row == 0, jnp.minimum(row, near_cap), row)
        for e in range(1, PLANES):
            mine = bits_col == e
            filled = jnp.sum(jnp.where(mine, jnp.minimum(col, level), 0.0), axis=0, keepdims=True)
            fits = (filled <= float(plan.far)) & (level[0:1, :] <= float(plan.each))
            limit = jnp.sum(jnp.where(fits, 1.0, 0.0), axis=1, keepdims=True) - 1.0
            out_col = jnp.where(mine, jnp.minimum(col, limit), out_col)
            out_row = jnp.where(bits_row == e, jnp.minimum(row, limit), out_row)
        return out_col, out_row

    half_col = jnp.where(bits_col == 0, all_col, jnp.floor((all_col + 1.0) * 0.5))
    half_row = jnp.where(bits_row == 0, all_row, jnp.floor((all_row + 1.0) * 0.5))
    first_col, first_row = wave(half_col, half_row, float(plan.near_cap))
    second_col, second_row = wave(all_col - first_col, all_row - first_row, 0.0)
    third_row = all_row - first_row - second_row

    def starts(row):
        ahead = (iota((n_own, n_own), 1) < iota((n_own, n_own), 0)) & (bits_row == bits_col)
        return jnp.sum(jnp.where(ahead, row, 0.0), axis=1, keepdims=True)

    by_rank = of_token(ranks)
    straight = early & (by_rank < of_token(direct_col))
    rank = by_rank - of_token(direct_col)
    first_n = of_token(first_col)
    second_n = of_token(second_col)
    e_token = (owners[...] // size) ^ plane
    in_first = ~straight & (rank < first_n)
    in_third = ~straight & (rank >= first_n + second_n)
    in_second = ~(straight | in_first | in_third)
    stride = (e_token - 1) * FAR_STRIDE
    first_at = stride + (of_token(starts(first_row)) + rank).astype(I32)
    second_at = stride + (of_token(starts(second_row)) + rank - first_n).astype(I32)
    third_at = owners[...] * cap + (rank - first_n - second_n).astype(I32)
    near_at = ((owners[...] % size) ^ (me[0] % size)) * plan.near_cap + rank.astype(I32)
    place[...] = jnp.full(place.shape, -1, I32)
    place[0:1, :] = jnp.where(in_first & (e_token > 0), first_at, -1)
    place[1:2, :] = jnp.where(in_first & (e_token == 0), near_at, -1)
    place[2:3, :] = jnp.where(in_second, second_at, -1)
    place[3:4, :] = jnp.where(straight, owners[...] * plan.direct + by_rank.astype(I32), -1)
    place[4:5, :] = jnp.where(in_third, third_at, -1)

    at_rank = (iota((wide, rows), 0).astype(F32) == by_rank).astype(F32).astype(BF16)
    high = (lists[...] // 64).astype(F32)
    low = (lists[...] % 64).astype(F32)

    def by_owner(values):
        picked = jnp.where(hot, values, 0.0).astype(BF16)
        return lax.dot_general(picked, at_rank, (((1,), (1,)), ((), ())), preferred_element_type=F32)

    live = by_owner(jnp.ones_like(high))
    ids = by_owner(high) * 64.0 + by_owner(low)
    step = jnp.max(third_row, axis=1, keepdims=True)
    for base in range(0, 2 * plan.sent, plan.sent):
        sent[:, base : base + wide] = jnp.where(live > 0.5, ids, -1.0).astype(I32)[:n_dp, :]
        start = base + wide
        for row in (direct_row, first_row, second_row):
            sent[:, start : start + n_own] = jnp.broadcast_to(row.astype(I32), (n_dp, n_own))
            start += n_own
        sent[:, start : start + LANES] = jnp.broadcast_to(step.astype(I32), (n_dp, LANES))


def route(plan, me, owners, lists):
    rows = owners.shape[1]
    return pl.pallas_call(
        functools.partial(route_kernel, plan),
        grid_spec=pltpu.PrefetchScalarGridSpec(
            num_scalar_prefetch=1,
            grid=(1,),
            in_specs=[pl.BlockSpec((1, rows), lambda i, m: (0, 0))] * 2,
            out_specs=(
                pl.BlockSpec((8, rows), lambda i, m: (0, 0)),
                pl.BlockSpec((plan.n_dp, 2 * plan.sent), lambda i, m: (0, 0)),
            ),
        ),
        out_shape=(
            jax.ShapeDtypeStruct((8, rows), I32),
            jax.ShapeDtypeStruct((plan.n_dp, 2 * plan.sent), I32),
        ),
        compiler_params=params(32),
        cost_estimate=pl.CostEstimate(
            flops=2 * rows * rows * plan.n_own, bytes_accessed=rows * 64, transcendentals=0
        ),
        name="route",
    )(me, owners, lists)


def slot_kernel(plan, me, heard, table, direct, near, first, second, third, counts):
    size = plan.plane
    wide, n_own = plan.wide, plan.n_own
    plane = me[0] // size
    owner = iota((plan.n_dp, n_own), 1)

    def listed(wave):
        return heard[:, wide + wave * n_own : wide + (wave + 1) * n_own]

    def mine(wave):
        return jnp.sum(jnp.where(owner == me[0], listed(wave), 0), axis=1, keepdims=True)

    def skip(slots, count):
        shift = 1
        while shift < wide:
            moved = pltpu.roll(slots, wide - shift, 1)
            slots = jnp.where((count // shift) % 2 == 1, moved, slots)
            shift *= 2
        return slots

    def of_bits(values, e):
        picked = jnp.zeros((size, values.shape[1]), I32)
        for q in range(PLANES):
            picked = jnp.where((plane ^ e) == q, values[q * size : (q + 1) * size, :], picked)
        return picked

    def by_distance(part, i):
        picked = iota((size, 1), 0) == ((me[0] % size) ^ i)
        return jnp.sum(jnp.where(picked, part, 0), axis=0, keepdims=True)

    n_direct, n_first, n_second = mine(0), mine(1), mine(2)
    total = jnp.sum(jnp.where(heard[:, :wide] >= 0, 1, 0), axis=1, keepdims=True)
    lane = iota((plan.n_dp, wide), 1)
    slots = table[...]
    direct[...] = jnp.where(lane < n_direct, slots, -1)
    slots = skip(slots, n_direct)
    in_first = jnp.where(lane < n_first, slots, -1)
    slots = skip(slots, n_first)
    in_second = jnp.where(lane < n_second, slots, -1)
    slots = skip(slots, n_second)
    third[...] = jnp.where(lane < total - n_direct - n_first - n_second, slots, -1)
    for i in range(size):
        near[i : i + 1, :] = by_distance(of_bits(in_first, 0), i)
    source = iota((plan.n_dp, 1), 0)
    for wave, values, out in ((0, in_first, first), (1, in_second, second)):
        for e in range(1, PLANES):
            part = of_bits(values, e)
            for i in range(size):
                at = i * (PLANES - 1) + e - 1
                out[at : at + 1, :] = by_distance(part, i)
            from_me = source == (plane ^ e) * size + me[0] % size
            at = wave * 4 + e - 1
            counts[at : at + 1, :] = jnp.sum(
                jnp.where(from_me, listed(1 + wave), 0), axis=0, keepdims=True
            )


def wave_slots(plan, me, heard, table):
    size = plan.plane
    shapes = [
        (plan.n_dp, plan.wide),
        (size, plan.wide),
        (size * (PLANES - 1), plan.wide),
        (size * (PLANES - 1), plan.wide),
        (plan.n_dp, plan.wide),
        (8, plan.n_own),
    ]
    return pl.pallas_call(
        functools.partial(slot_kernel, plan),
        grid_spec=pltpu.PrefetchScalarGridSpec(
            num_scalar_prefetch=1,
            grid=(1,),
            in_specs=[
                pl.BlockSpec((plan.n_dp, plan.sent), lambda i, m: (0, 0)),
                pl.BlockSpec((plan.n_dp, plan.wide), lambda i, m: (0, 0)),
            ],
            out_specs=tuple(pl.BlockSpec(shape, lambda i, m: (0, 0)) for shape in shapes),
        ),
        out_shape=tuple(jax.ShapeDtypeStruct(shape, I32) for shape in shapes),
        compiler_params=params(32),
        cost_estimate=HIDDEN,
        name="wave_slots",
    )(me, heard, table)


def combine(own, other, keys):
    rows, width = keys.shape
    tile = fit(rows, 128)

    @pl.loop(0, rows // tile)
    def _(i):
        at = pl.ds(pl.multiple_of(i * tile, tile), tile)
        parts = own[at, width:].astype(F32) + other[at, width:].astype(F32)
        energy = jnp.sum(parts, axis=1, keepdims=True)
        scale = lax.rsqrt(energy * (1.0 / D) + EPSILON)
        terms = own[at, :width].astype(F32) + other[at, :width].astype(F32)
        keys[at, :] = jnp.where(scale > 0.0, terms * scale, 0.0).astype(BF16)


def permute(line, first, place, chunks, out):
    total = None
    start = 0
    for keys in chunks:
        rows = keys.shape[0]
        places = place[line : line + 1, start : start + rows]
        start += rows
        onehot = (iota((out.shape[0], rows), 0) + first == places).astype(F32).astype(BF16)
        part = jnp.dot(onehot, keys[...], preferred_element_type=F32)
        total = part if total is None else total + part
    out[...] = total.astype(BF16)


def pack_kernel(moves, n_keys, fresh, place, *refs):
    chunks = refs[:n_keys]
    if fresh:
        own, other = refs[n_keys : n_keys + 2]
        outs, keys = refs[n_keys + 2 : -1], refs[-1]
        combine(own, other, keys)
        chunks = (*chunks, keys)
    else:
        outs = refs[n_keys:]
    for (line, first, _), out in zip(moves, outs):
        permute(line, first, place, chunks, out)


def pack(moves, place, keys, fresh=()):
    width = keys[0].shape[1] if keys else fresh[0].shape[1] - 2 * LANES
    sizes = [size for _, _, size in moves] + [part.shape[0] for part in fresh[:1]]
    rows = place.shape[1]
    whole = lambda i: (0, 0)
    operands = [place, *keys, *fresh]
    return list(
        pl.pallas_call(
            functools.partial(pack_kernel, moves, len(keys), bool(fresh)),
            grid=(1,),
            in_specs=[pl.BlockSpec(part.shape, whole) for part in operands],
            out_specs=tuple(pl.BlockSpec((size, width), whole) for size in sizes),
            out_shape=tuple(jax.ShapeDtypeStruct((size, width), BF16) for size in sizes),
            compiler_params=params(60),
            cost_estimate=HIDDEN,
            name="pack_keys",
        )(*operands)
    )


def spread_kernel(plan, wave, me, counts, *refs):
    size = plan.plane
    outs = refs[len(refs) - size :]
    refs = refs[: len(refs) - size]
    cap = plan.each
    base = (me[0] // size) * size
    for e in range(1, PLANES):
        rows = refs[e - 1]
        row = iota((cap, rows.shape[0]), 0)
        column = iota(row.shape, 1)
        at = wave * 4 + e - 1
        hits = []
        for k in range(size):
            owner = (me[0] % size) ^ k
            start = lax.fori_loop(0, owner, lambda i, total: total + counts[at, base + i], 0)
            hit = (column == row + start) & (row < counts[at, base + owner])
            hits.append(hit.astype(F32).astype(BF16))
        moved = jnp.dot(
            jnp.concatenate(hits, axis=0), rows[...], preferred_element_type=F32
        ).astype(BF16)
        for k in range(size):
            outs[k][(e - 1) * cap : e * cap, :] = moved[k * cap : (k + 1) * cap, :]


def spread(plan, wave, me, counts, packed):
    width = packed[0].shape[1]
    each = (PLANES - 1) * plan.each
    whole = lambda i, m, c: (0, 0)
    return list(
        pl.pallas_call(
            functools.partial(spread_kernel, plan, wave),
            grid_spec=pltpu.PrefetchScalarGridSpec(
                num_scalar_prefetch=2,
                grid=(1,),
                in_specs=[pl.BlockSpec(block.shape, whole) for block in packed],
                out_specs=(pl.BlockSpec((each, width), whole),) * plan.plane,
            ),
            out_shape=(jax.ShapeDtypeStruct((each, width), BF16),) * plan.plane,
            compiler_params=params(60),
            cost_estimate=HIDDEN,
            name="spread_rows",
        )(me, counts, *packed)
    )


def centre_kernel(n_in, slots, lists, centroids, out, table, placed):
    step = pl.program_id(0)
    block = centroids.shape[0]
    n_lists = n_in * block
    chunks = centroids.shape[1] // LANES
    count = placed.shape[0] // chunks
    size = out.shape[0]

    @pl.when(step == 0)
    def _():
        table[pl.ds(n_lists * chunks, chunks), :] = jnp.zeros((chunks, LANES), F32)

    @pl.when(step < n_in)
    def _():
        @pl.loop(0, block // 16)
        def _(i):
            wide = centroids[pl.ds(pl.multiple_of(i * 16, 16), 16), :].astype(F32)
            for top in range(0, 16, 8):
                first = (step * block + i * 16 + top) * chunks
                for c in range(chunks):
                    part = wide[top : top + 8, c * LANES : (c + 1) * LANES]
                    table[pl.ds(first + c, 8, stride=chunks), :] = part

    @pl.when(step == n_in)
    def _():
        @pl.loop(0, count // 16)
        def _(i):
            found = []
            for u in range(16):
                a = i * 16 + u
                row = table[pl.ds(pl.multiple_of(lists[a], chunks), chunks), :]
                found.append((slots[a], row))
            for at, row in found:
                placed[pl.ds(pl.multiple_of(at, chunks), chunks), :] = -row

    @pl.when(step >= n_in)
    def _():
        @pl.loop(0, size // 16)
        def _(i):
            rows = []
            for top in range(0, 16, 8):
                first = ((step - n_in) * size + i * 16 + top) * chunks
                rows.append(
                    jnp.concatenate(
                        [placed[pl.ds(first + c, 8, stride=chunks), :] for c in range(chunks)], axis=1
                    )
                )
            out[pl.ds(pl.multiple_of(i * 16, 16), 16), :] = jnp.concatenate(rows, axis=0).astype(BF16)


def centres(slots, lists, centroids):
    count = slots.shape[0]
    n_lists, width = centroids.shape
    slots = slots * (width // LANES)
    lists = jnp.where(lists < 0, n_lists, lists) * (width // LANES)
    block, size = fit(n_lists, 512), fit(count, 512)
    n_in = n_lists // block
    chunks = width // LANES
    return pl.pallas_call(
        functools.partial(centre_kernel, n_in),
        grid_spec=pltpu.PrefetchScalarGridSpec(
            num_scalar_prefetch=2,
            grid=(n_in + count // size,),
            in_specs=[pl.BlockSpec((block, width), lambda i, s, l: (jnp.minimum(i, n_in - 1), 0))],
            out_specs=pl.BlockSpec((size, width), lambda i, s, l: (jnp.maximum(i - n_in, 0), 0)),
            scratch_shapes=[
                pltpu.VMEM(((n_lists + 1) * chunks, LANES), F32),
                pltpu.VMEM((count * chunks, LANES), F32),
            ],
        ),
        out_shape=jax.ShapeDtypeStruct((count, width), BF16),
        compiler_params=params(60),
        cost_estimate=HIDDEN,
        name="centroid_rows",
    )(slots, lists, centroids)


def place_kernel(sizes, slots, before, *refs):
    parts, out, arrived, sems = refs[: len(sizes)], *refs[len(sizes) :]
    tile = out.shape[0]
    step = pl.program_id(0)
    first = step * tile

    @pl.when(step == 0)
    def _():
        copies = []
        start = 0
        for i, (part, size) in enumerate(zip(parts, sizes)):
            copies.append(pltpu.make_async_copy(part, arrived.at[pl.ds(start, size)], sems.at[i]))
            start += size
        for copy in copies:
            copy.start()
        for copy in copies:
            copy.wait()

    onehot = (slots[...] == iota((tile, slots.shape[1]), 0) + first).astype(F32).astype(BF16)
    keys = jnp.dot(onehot, arrived[...], preferred_element_type=F32)
    out[...] = (keys + before[...].astype(F32)).astype(BF16)


def place_rows(slots, arrived, before):
    count, width = before.shape
    sizes = [part.shape[0] for part in arrived]
    n_rows = sum(sizes)
    tile = fit(count, 512)
    return pl.pallas_call(
        functools.partial(place_kernel, sizes),
        grid=(count // tile,),
        in_specs=[
            pl.BlockSpec((1, n_rows), lambda i: (0, 0)),
            pl.BlockSpec((tile, width), lambda i: (i, 0)),
        ]
        + [pl.BlockSpec(memory_space=pl.ANY)] * len(sizes),
        out_specs=pl.BlockSpec((tile, width), lambda i: (i, 0)),
        out_shape=jax.ShapeDtypeStruct((count, width), BF16),
        scratch_shapes=[
            pltpu.VMEM((n_rows, width), BF16),
            pltpu.SemaphoreType.DMA((len(sizes),)),
        ],
        compiler_params=params(60),
        cost_estimate=HIDDEN,
        name="residual_rows",
    )(slots, before, *arrived)


def up16(value):
    return -(-value // 16) * 16


class Plan:
    def __init__(self, n_dp, rows, cap):
        self.n_dp, self.cap = n_dp, cap
        self.plane = n_dp // PLANES
        self.n_own = -(-n_dp // LANES) * LANES
        self.wide = -(-(cap + 1) // LANES) * LANES
        self.sent = self.wide + 3 * self.n_own + LANES
        self.early = rows // 2
        self.direct = up16(cap // 3)
        self.each = up16(cap // 3)
        self.near_cap = min(cap, up16(cap * 2 // 3))
        self.far = up16(rows * 5 // 32)


def shards(hidden, norm_gain, projection, centroids, owners, local_list, slot_table):
    n_dp = lax.axis_size("dp")
    me = lax.axis_index("tp").astype(I32)
    here = lax.axis_index("dp").astype(I32)
    rows = owners.shape[0]
    width = projection.shape[1]
    cap = slot_table.shape[1] // n_dp
    plan = Plan(n_dp, rows, cap)
    size = plan.plane
    gain = norm_gain.reshape(1, -1)
    groups = [list(range(q * size, (q + 1) * size)) for q in range(PLANES)]
    here = here.reshape(1)

    def across(blocks):
        pieces = len(blocks) // (PLANES - 1)
        return [
            lax.ppermute(
                block,
                "dp",
                [(p, ((p // size) ^ (1 + i // pieces)) * size + p % size) for p in range(n_dp)],
            )
            for i, block in enumerate(blocks)
        ]

    def exchange(blocks):
        return [blocks[0]] + [
            lax.ppermute(block, "dp", [(p, p - p % size + (p % size ^ k)) for p in range(n_dp)])
            for k, block in enumerate(blocks)
            if k > 0
        ]

    place, sent = route(plan, here, owners.reshape(1, rows), local_list.reshape(1, rows))
    heard = lax.all_to_all(
        sent.reshape(2 * n_dp, plan.sent), ("dp", "tp"), split_axis=0, concat_axis=0, tiled=True
    )
    def partials(chunk):
        half = rows // 2
        for_other = partial_keys((2 - 2 * me + chunk).reshape(1), hidden, gain, projection, half)
        other = lax.ppermute(for_other, "tp", [(0, 1), (1, 0)])
        own = partial_keys((2 * me + chunk).reshape(1), hidden, gain, projection, half)
        return own, other

    def direct(block):
        block = block.reshape(n_dp, -1, width)
        got = lax.all_to_all(block, "dp", split_axis=0, concat_axis=0, tiled=True)
        return got.reshape(-1, width)

    def fars(line):
        return [(line, e * FAR_STRIDE, plan.far) for e in range(PLANES - 1)]

    early_place = place[:, : plan.early]
    straight, early = pack([(3, 0, n_dp * plan.direct)], early_place, [], partials(0))
    straight = direct(straight)
    *far_first, late = pack(fars(0), place, [early], partials(1))
    far_first = across(far_first)
    nears = [(1, k * plan.near_cap, plan.near_cap) for k in range(size)]
    packed = pack(nears + fars(2), place, [early, late])
    near = exchange(packed[:size])
    far_second = across(packed[size:])

    level = jnp.max(heard[:, -1])
    heard = lax.dynamic_index_in_dim(heard.reshape(n_dp, 2, plan.sent), me, 1, keepdims=False)
    lists = heard[:, :cap].reshape(n_dp * cap)
    table = jnp.pad(slot_table.reshape(n_dp, cap), ((0, 0), (0, plan.wide - cap)))
    direct_slots, near_slots, first_slots, second_slots, third_slots, counts = wave_slots(
        plan, here, heard, table
    )
    centre = centres(slot_table.reshape(-1), lists, centroids)

    def flat(*parts):
        parts = [slots[:, :each].reshape(1, -1) for slots, each in parts]
        return jnp.concatenate(parts, axis=1) if len(parts) > 1 else parts[0]

    far_first, near, centre = lax.optimization_barrier((far_first, near, centre))
    passed = exchange(spread(plan, 0, here, counts, far_first))
    slots = flat((direct_slots, plan.direct), (near_slots, plan.near_cap))
    out = place_rows(slots, [straight, *near], centre)
    far_second, out = lax.optimization_barrier((far_second, out))
    blocks = spread(plan, 1, here, counts, far_second)
    blocks, passed = lax.optimization_barrier((blocks, passed))
    late_passed = exchange(blocks)
    slots = flat((first_slots, plan.each), (second_slots[: PLANES - 1], plan.each))
    out = place_rows(slots, [*passed, blocks[0]], out)
    slots = flat((second_slots[PLANES - 1 :], plan.each))

    def finish(args):
        return place_rows(args["slots"], args["rows"], args["out"])

    def finish_more(size):
        def branch(args):
            third = args["place"][4:5]
            third = jnp.where(third < 0, -1, third // cap * size + third % cap)
            third = jnp.broadcast_to(third, args["place"].shape)
            (more,) = pack([(0, 0, n_dp * size)], third, args["keys"])
            return place_rows(flat((args["third_slots"], size)), [direct(more)], finish(args))

        return branch

    few = up16(cap // 3)
    return lax.switch(
        (level > 0).astype(I32) + (level > few).astype(I32),
        [finish, finish_more(few), finish_more(cap)],
        dict(
            slots=slots, rows=late_passed[1:], out=out, place=place, keys=[early, late],
            third_slots=third_slots,
        ),
    )


def solution(mesh):
    placed = (
        P("dp", "tp"),
        P("tp"),
        P("tp", None),
        P("dp", None),
        P(("dp", "tp"), None),
        P(("dp", "tp")),
        P(("dp", "tp"), None),
    )
    return jax.shard_map(
        shards, mesh=mesh, in_specs=placed, out_specs=P(("dp", "tp"), None), check_vma=False
    )
```
